512 devices in a mesh: seq: 8 (over z_lo), exp: 64 (over x, z_hi, y, core).
Axes of the slice: x: 4, y: 4, z: 16 (z_hi: 2, z_lo: 8; z = z_hi * 8 + z_lo), core: 2. Of those that a mesh axis runs over, the one named last changes fastest.
Arguments:
- queries: bfloat16 [64, 512, 4096], P('exp', 'seq'), may hold values from -160 to 160
- key_heads: bfloat16 [64, 512, 512], P('exp', 'seq'), may hold values from -4 to 4
- value_heads: bfloat16 [64, 512, 512], P('exp', 'seq'), may hold values from -4 to 4
- doc_ids: int32 [64, 512], P('exp'), may hold values from 0 to 7, never falling along the last dimension, each value on 1 to 256 neighbouring positions
- residual: bfloat16 [64, 512, 2048], P('exp', 'seq'), may hold values from -10 to 10
- w_out: bfloat16 [4096, 2048], P('seq'), may hold values from -0.375 to 0.375
- norm_gain: float32 [2048], replicated, may hold values from 0.1 to 1.9
- router_logits: float32 [64, 512, 64], P('exp', 'seq'), may hold values from -12 to 305
- expert_ids: int32 [64, 512, 8], P('exp', 'seq'), may hold values from 0 to 63, as said below
- keep_mask: int32 [64, 512, 8], P('exp', 'seq'), may hold values from 0 to 1, as said below
- w_gate: bfloat16 [64, 768, 2048], P('exp', 'seq'), may hold values from -0.125 to 0.125
- w_up: bfloat16 [64, 768, 2048], P('exp', 'seq'), may hold values from -0.125 to 0.125
- w_down: bfloat16 [64, 768, 2048], P('exp', 'seq'), may hold values from -0.21875 to 0.21875
Outputs:
- hidden: bfloat16 [64, 512, 2048], P('exp', 'seq')
- expert_out: bfloat16 [64, 512, 2048], P('exp', 'seq')
The draws below stay inside these ranges and needn't reach their ends.
Inputs may be any that keep to these rules, and one draw needn't show every extreme that they name: `expert_ids`: each token names 8 different experts. `keep_mask`: take the assignments of one device's 64 positions of a sequence in order of position and then along the last dimension: an assignment is kept exactly when fewer than 8 earlier ones of that device name the same expert. So at most 8 kept assignments of one device name one expert; other experts may have fewer. In every draw there is an expert, the same one for all devices, that has exactly 8 kept assignments from every device.
All inputs are finite; a program needn't handle non-finite values.
Results may differ from the reference program's by a relative error of at most 0.029.
Values may be sent and summed in bfloat16 or wider, within the bound.
A program may use at most 64 MiB of HBM per device.

```python
import math
import jax
import jax.numpy as jnp
import numpy as np
from jax import lax

D = 2048
QH = 32
KVH = 4
HD = 128
EXPERT_FF = 768
TOPK = 8
DOCS = 8
TOK_DEV = 64
LEN = 512
SEQS = 64
EXPERT_COUNT = 64
CAP = 8
N_SEQ = 8


def key_numbers(key):
    base_field = jnp.clip(jax.random.normal(jax.random.fold_in(key, 31), (SEQS, LEN, KVH, HD), jnp.float32), -4.0, 4.0)
    return base_field


def routing(key):
    key = jax.random.fold_in(key, 41)
    total_rows = SEQS * LEN
    blocks = total_rows // TOK_DEV
    expert_span_indices = jnp.arange(EXPERT_COUNT, dtype=jnp.int32)
    favored = jax.random.randint(jax.random.fold_in(key, 1), (), 0, EXPERT_COUNT, dtype=jnp.int32)
    extra_score_term = jax.random.randint(jax.random.fold_in(key, 2), (EXPERT_COUNT,), 0, 2048, dtype=jnp.int32)
    noise_component = jax.random.randint(jax.random.fold_in(key, 3), (total_rows, EXPERT_COUNT), 0, 4096, dtype=jnp.int32)
    leading_rows = (jnp.arange(total_rows, dtype=jnp.int32) % TOK_DEV < CAP)[:, None] & (expert_span_indices[None, :] == favored)
    score_values = (noise_component + extra_score_term[None, :] + jnp.where(leading_rows, 8192, 0)) * EXPERT_COUNT + expert_span_indices[None, :]
    chosen = lax.top_k(score_values, TOPK)[1].astype(jnp.int32)
    grouped = chosen.reshape(blocks, TOK_DEV * TOPK)
    onehot = (grouped[:, :, None] == expert_span_indices).astype(jnp.int32)
    before = jnp.cumsum(onehot, axis=1, dtype=jnp.int32) - onehot
    rank_index = jnp.sum(before * onehot, axis=-1, dtype=jnp.int32)
    kept_flag = (rank_index < CAP).astype(jnp.int32).reshape(total_rows, TOPK)
    return (chosen, kept_flag)


def draw_key_heads(key, part):
    base_field = key_numbers(key)
    result_field = base_field
    return result_field.reshape(SEQS, LEN, KVH * HD).astype(jnp.bfloat16)


def draw_queries(key, part):
    key = jax.random.fold_in(key, 2)
    grid_shape = (SEQS, LEN, KVH, QH // KVH, HD)
    result_field = jnp.clip(jax.random.normal(key, grid_shape, jnp.float32), -4.0, 4.0)
    return result_field.reshape(SEQS, LEN, QH * HD).astype(jnp.bfloat16)


def draw_router_logits(key, part):
    key = jax.random.fold_in(key, 3)
    return 3.0 * jnp.clip(jax.random.normal(key, (SEQS, LEN, EXPERT_COUNT), jnp.float32), -4.0, 4.0)


def draw_residual(key, part):
    key = jax.random.fold_in(key, 4)
    row_scale = jnp.exp(jax.random.uniform(jax.random.fold_in(key, 1), (SEQS, LEN, 1), jnp.float32, jnp.log(0.15), jnp.log(1.5)))
    col_scale = jnp.exp(jax.random.uniform(jax.random.fold_in(key, 2), (1, 1, D), jnp.float32, jnp.log(0.15), jnp.log(1.5)))
    values = jnp.clip(jax.random.normal(key, (SEQS, LEN, D), jnp.float32), -4.0, 4.0)
    return (values * row_scale * col_scale).astype(jnp.bfloat16)


def draw_expert_ids(key, part):
    chosen, kept_flag = routing(key)
    return chosen.reshape(SEQS, LEN, TOPK)


def draw_keep_mask(key, part):
    chosen, kept_flag = routing(key)
    return kept_flag.reshape(SEQS, LEN, TOPK)


def levels(own_key, extent, cuts, least, largest):
    gain = 1.0
    for dim, shards_of in cuts:
        draws = jax.random.uniform(jax.random.fold_in(jax.random.fold_in(own_key, 6), dim), (shards_of,), jnp.float32, least / len(cuts), largest / len(cuts))
        gain = gain * jnp.repeat(jnp.exp(draws), extent[dim] // shards_of).reshape((-1,) + (1,) * (len(extent) - 1 - dim))
    return gain


def split_up(amount, total, bound, slope):
    loads = [(1 << 20) // math.isqrt(grade ** slope) + 1 for grade in range(2, amount + 1)]
    spare, given = total - bound - (amount - 1), [1] * (amount - 1)
    while spare > 0:
        movable = [i for i in range(amount - 1) if given[i] < bound]
        mass, remaining = sum([loads[i] for i in movable]), spare
        for i in movable:
            extra = min(bound - given[i], max(1, remaining * loads[i] // mass), spare)
            given[i] = given[i] + extra
            spare = spare - extra
    return np.array([bound] + given)


def uneven(stream_key, count, total, limit, slope):
    if count == 2:
        one = jax.random.randint(stream_key, (), max(1, total - limit), min(limit, total - 1) + 1)
        return jnp.stack([one, total - one])
    sizes = jnp.asarray(split_up(count, total, limit, slope), jnp.int32)
    twos = (count - 1) // 2
    source_of, sink = sizes[1:1 + 2 * twos:2], sizes[2:2 + 2 * twos:2]
    margin = jnp.minimum(source_of - 1, limit - sink)
    moved = jax.random.randint(jax.random.fold_in(stream_key, 1), (twos,), 0, 1 << 20) % (margin + 1)
    sizes = sizes.at[1:1 + 2 * twos:2].set(source_of - moved).at[2:2 + 2 * twos:2].set(sink + moved)
    return sizes[jax.random.permutation(jax.random.fold_in(stream_key, 2), count)]


def noise(key, shape, scale, bound, shards=(), kind=jnp.bfloat16):
    values = scale * jax.random.normal(key, shape, jnp.float32)
    if shards:
        values = values * levels(key, shape, shards, -0.22, 0.18)
    return jnp.clip(values, -bound, bound).astype(kind)


def setup_inputs(seed: int = 0) -> dict:
    streams_of = jax.random.split(jax.random.key(seed), 14)
    queries = draw_queries(jax.random.fold_in(streams_of[13], 71), 0)
    key_heads = draw_key_heads(jax.random.fold_in(streams_of[13], 71), 0)
    value_heads = noise(streams_of[2], (SEQS, LEN, KVH * HD), 1.0, 4.0, ((0, 64), (1, 8)))
    doc_ids = jax.vmap(lambda own: jnp.searchsorted(jnp.cumsum(uneven(own, DOCS, LEN, LEN // 2, 2)), jnp.arange(LEN), side="right"))(jax.random.split(streams_of[3], SEQS)).reshape((SEQS, LEN)).astype(jnp.int32)
    residual = draw_residual(jax.random.fold_in(streams_of[13], 71), 0)
    w_out = noise(streams_of[5], (QH * HD, D), (QH * HD // 16) ** -0.5, 0.375, ((0, 8),))
    norm_gain = jnp.clip(1.0 + 0.18 * jax.random.normal(streams_of[6], (D,), jnp.float32), 0.1, 1.9)
    router_logits = draw_router_logits(jax.random.fold_in(streams_of[13], 71), 0)
    expert_ids = draw_expert_ids(jax.random.fold_in(streams_of[13], 71), 0)
    keep_mask = draw_keep_mask(jax.random.fold_in(streams_of[13], 71), 0)
    w_gate = noise(streams_of[10], (EXPERT_COUNT, EXPERT_FF, D), D ** -0.5, 0.125, ((0, 64), (1, 8)))
    w_up = noise(streams_of[11], (EXPERT_COUNT, EXPERT_FF, D), D ** -0.5, 0.125, ((0, 64), (1, 8)))
    w_down = noise(streams_of[12], (EXPERT_COUNT, EXPERT_FF, D), EXPERT_FF ** -0.5, 0.21875, ((0, 64), (1, 8)))
    return dict(queries=queries, key_heads=key_heads, value_heads=value_heads, doc_ids=doc_ids, residual=residual, w_out=w_out, norm_gain=norm_gain, router_logits=router_logits, expert_ids=expert_ids, keep_mask=keep_mask, w_gate=w_gate, w_up=w_up, w_down=w_down)


epsilon = 1e-06

def attention_block(queries, key_heads, value_heads, doc_ids):
    length = queries.shape[0]
    group_size = QH // KVH
    q_grid = queries.astype(jnp.float32).reshape(length, KVH, group_size, HD)
    k_grid = key_heads.astype(jnp.float32).reshape(length, KVH, HD)
    v_grid = value_heads.astype(jnp.float32).reshape(length, KVH, HD)
    score_values = jnp.einsum('qhgd,khd->hgqk', q_grid, k_grid) * (1.0 / HD ** 0.5)
    position = jnp.arange(length, dtype=jnp.int32)
    allowed = (position[None, :] <= position[:, None]) & (doc_ids[None, :] == doc_ids[:, None])
    score_values = jnp.where(allowed, score_values, -jnp.inf)
    top_score = lax.optimization_barrier(jnp.max(score_values, axis=-1, keepdims=True))
    exp_terms = jnp.exp(score_values - top_score)
    prob_rows = (exp_terms / lax.optimization_barrier(jnp.sum(exp_terms, axis=-1, keepdims=True))).astype(jnp.bfloat16)
    attended = jnp.einsum('hgqk,khd->qhgd', prob_rows.astype(jnp.float32), v_grid)
    return attended.reshape(length, QH * HD).astype(jnp.bfloat16)

def project(attended, w_out):
    group_width = QH * HD // N_SEQ
    accum = jnp.zeros((attended.shape[0], w_out.shape[1]), jnp.float32)
    for group_index in range(N_SEQ):
        lo_col = group_index * group_width
        partial_value = jnp.dot(attended[:, lo_col:lo_col + group_width], w_out[lo_col:lo_col + group_width], preferred_element_type=jnp.float32)
        rounded = lax.optimization_barrier(partial_value.astype(jnp.bfloat16))
        accum = accum + rounded.astype(jnp.float32)
    return accum

def kept_slots(id_flat, keep_flat):
    total_rows = id_flat.shape[0]
    blocks = total_rows // TOK_DEV
    expert_span_indices = jnp.arange(EXPERT_COUNT, dtype=jnp.int32)
    grouped = id_flat.reshape(blocks, TOK_DEV * TOPK)
    kept_flag = keep_flat.reshape(blocks, TOK_DEV * TOPK)
    onehot = ((grouped[:, :, None] == expert_span_indices) & (kept_flag[:, :, None] == 1)).astype(jnp.int32)
    before = jnp.cumsum(onehot, axis=1, dtype=jnp.int32) - onehot
    slot_index = lax.optimization_barrier(jnp.sum(before * onehot, axis=-1, dtype=jnp.int32))
    return slot_index.reshape(total_rows, TOPK).astype(jnp.int32)

def reference(queries, key_heads, value_heads, doc_ids, residual, w_out, norm_gain, router_logits, expert_ids, keep_mask, w_gate, w_up, w_down):

    def per_sequence(pieces):
        attended = attention_block(pieces[0], pieces[1], pieces[2], pieces[3])
        return pieces[4].astype(jnp.float32) + project(attended, w_out)
    hidden = lax.map(per_sequence, (queries, key_heads, value_heads, doc_ids, residual))
    square = lax.optimization_barrier(jnp.mean(hidden * hidden, axis=-1, keepdims=True))
    normed = (hidden * lax.rsqrt(square + epsilon) * norm_gain.astype(jnp.float32)).astype(jnp.bfloat16)
    total_rows = SEQS * LEN
    blocks = total_rows // TOK_DEV
    flat_rows = normed.reshape(total_rows, D)
    id_flat = expert_ids.reshape(total_rows, TOPK).astype(jnp.int32)
    keep_flat = keep_mask.reshape(total_rows, TOPK).astype(jnp.int32)
    chosen = jnp.take_along_axis(router_logits.reshape(total_rows, EXPERT_COUNT), id_flat, axis=1)
    exp_terms = jnp.exp(chosen - lax.optimization_barrier(jnp.max(chosen, axis=-1, keepdims=True)))
    gate_probs = exp_terms / lax.optimization_barrier(jnp.sum(exp_terms, axis=-1, keepdims=True))
    weights = (gate_probs * keep_flat.astype(jnp.float32)).astype(jnp.bfloat16)
    slot_index = kept_slots(id_flat, keep_flat)
    token_index = jnp.broadcast_to(jnp.arange(total_rows, dtype=jnp.int32)[:, None], (total_rows, TOPK))
    target = jnp.where(keep_flat == 1, id_flat, EXPERT_COUNT).astype(jnp.int32)
    column = (token_index // TOK_DEV * CAP + slot_index).astype(jnp.int32)
    row_table = jnp.full((EXPERT_COUNT, blocks * CAP), total_rows, jnp.int32).at[target, column].set(token_index, mode='drop')
    weight_table = jnp.zeros((EXPERT_COUNT, blocks * CAP), jnp.bfloat16).at[target, column].set(weights, mode='drop')
    padded = jnp.concatenate([flat_rows, jnp.zeros((1, D), jnp.bfloat16)], axis=0)

    def one_expert(accum, pieces):
        row_ids, row_weight, gate_w, up_w, down_w = pieces
        picked = padded[row_ids]
        gate_val = jnp.dot(picked, gate_w.T, preferred_element_type=jnp.float32)
        up_val = jnp.dot(picked, up_w.T, preferred_element_type=jnp.float32)
        act_rows = (jax.nn.silu(gate_val) * up_val).astype(jnp.bfloat16)
        produced = jnp.dot(act_rows, down_w, preferred_element_type=jnp.float32).astype(jnp.bfloat16)
        scaled = produced.astype(jnp.float32) * row_weight.astype(jnp.float32)[:, None]
        return (accum.at[row_ids].add(scaled, mode='drop'), None)
    accum = jnp.zeros((total_rows, D), jnp.float32)
    accum = lax.scan(one_expert, accum, (row_table, weight_table, w_gate, w_up, w_down))[0]
    return (hidden.astype(jnp.bfloat16), accum.reshape(SEQS, LEN, D).astype(jnp.bfloat16))
```

```python
import functools

import jax
import jax.numpy as jnp
from jax import lax
from jax.experimental import pallas as pl
from jax.experimental.pallas import tpu as pltpu
from jax.sharding import PartitionSpec as P

MESH = pl.DeviceIdType.MESH
HD = 128
CAP = 8
X, Y, Z, LINE, CORES = 4, 4, 16, 8, 2
PLANE = X * Y * CORES
SUB = 4
CHUNKS = 4
EPSILON = 1e-06
NEG = -1e30
ANY = pl.BlockSpec(memory_space=pl.ANY)
VMEM = pl.BlockSpec(memory_space=pltpu.VMEM)


def place():
    s = lax.axis_index("seq")
    e = lax.axis_index("exp")
    c = e % 2
    y = (e // 2) % Y
    zh = (e // (2 * Y)) % 2
    x = e // (4 * Y)
    return x, y, zh * LINE + s, c


def device(x, y, z, c):
    x, y, z = x % X, y % Y, z % Z
    return {"seq": z % LINE, "exp": ((x * 2 + z // LINE) * Y + y) * 2 + c}


def rows(start, count):
    return pl.ds(pl.multiple_of(start, 16), count)


def meet(peers):
    barrier = pltpu.get_barrier_semaphore()
    for peer in peers:
        pl.semaphore_signal(barrier, inc=1, device_id=peer, device_id_type=MESH)
    pl.semaphore_wait(barrier, len(peers))


Z_OFFSETS = (1, -1, 2, -2, 3, -3, 4)


def front_kernel(
    q_ref, k_ref, v_ref, bias_ref, res_ref, gain_ref, meta_ref, wout_ref, wg_ref, wu_ref, wd_ref,
    hidden_ref, normed_ref, wts_ref, metas_ref,
    wbuf, kv, att, total, send, recv, local,
):
    x, y, z, c = place()
    s = z % LINE
    p = z % SUB
    at = lambda dx=0, dy=0, dz=0: device(x + dx + X, y + dy + Y, z + dz + Z, c)
    sibling = device(x, y, z, 1 - c)
    counter = [0]

    def remote(src, dst, peer):
        i = counter[0]
        counter[0] += 1
        return pltpu.make_async_remote_copy(
            src_ref=src, dst_ref=dst, send_sem=send.at[i], recv_sem=recv.at[i],
            device_id=peer, device_id_type=MESH,
        )

    meet(
        [at(dz=d) for d in (1, -1, 2, -2, 3, -3, 4, -4, 8)]
        + [at(dx=1), at(dx=-1), at(dy=1), at(dy=-1), sibling]
    )

    pending = []
    kv[4, 0] = k_ref[...]
    kv[4, 1] = v_ref[...]
    kv_steps = [remote(kv.at[4 - d], kv.at[3 - d], at(dz=1)) for d in range(4)]
    kv_steps[0].start()

    ja = (y * 2 + c) * X + x
    jb = (x * 2 + c) * Y + y
    mine = jnp.where(s < 4, ja, jb) * 16
    piece = wbuf.at[s, rows(mine, 16)]
    own = pltpu.make_async_copy(wout_ref.at[rows(mine, 16)], piece, local.at[0])
    own.start()
    z_copies = [remote(wout_ref.at[rows(mine, 16)], piece, at(dz=d)) for d in Z_OFFSETS]
    for copy in z_copies:
        copy.start()
    zh = z // LINE
    metas_ref[0] = meta_ref[zh]
    meta_copies = [
        remote(meta_ref.at[1 - zh], metas_ref.at[3], at(dz=8)),
        remote(meta_ref.at[((z + 4) % Z) // LINE], metas_ref.at[1], at(dz=4)),
        remote(meta_ref.at[((z + 12) % Z) // LINE], metas_ref.at[2], at(dz=-4)),
    ]
    for copy in meta_copies:
        copy.start()
    for m, ref in enumerate((wg_ref, wu_ref, wd_ref)):
        pltpu.make_async_copy(ref, wts_ref.at[m, rows(96 * p, 96)], local.at[1 + m]).start()
    for m, ref in enumerate((wg_ref, wu_ref, wd_ref)):
        pltpu.make_async_copy(ref, wts_ref.at[m, rows(96 * p, 96)], local.at[1 + m]).wait()
    kv_steps[0].wait_recv()
    kv_steps[1].start()
    own.wait()
    for copy in z_copies:
        copy.wait_recv()

    def block(owner):
        return wts_ref.at[:, rows(96 * ((owner + SUB) % SUB), 96)]

    up1 = remote(block(p), block(p), at(dz=1))
    down1 = remote(block(p), block(p), at(dz=-1))
    up2 = remote(block(p - 1), block(p - 1), at(dz=1))
    down2 = remote(block(p + 1), block(p + 1), at(dz=-1))

    def ring(region, lo, step):
        first = [remote(region(0, lo, 4), region(0, lo, 4), step(d)) for d in (1, -1)]
        second = [
            remote(region(-1, lo, 2), region(-1, lo, 2), step(1)),
            remote(region(1, lo + 2, 2), region(1, lo + 2, 2), step(-1)),
        ]
        return first, second

    def region_ax(d, lo, n):
        return wbuf.at[pl.ds(lo, n), rows(16 * ((y * 2 + c) * X + (x + d + X) % X), 16)]

    def region_by(d, lo, n):
        return wbuf.at[pl.ds(lo, n), rows(16 * ((x * 2 + c) * Y + (y + d + Y) % Y), 16)]

    def region_ay(d, lo, n):
        return wbuf.at[pl.ds(lo, n), rows(64 * (((y + d + Y) % Y) * 2 + c), 64)]

    def region_bx(d, lo, n):
        return wbuf.at[pl.ds(lo, n), rows(64 * (((x + d + X) % X) * 2 + c), 64)]

    step_x = lambda d: at(dx=d)
    step_y = lambda d: at(dy=d)
    a1, a2 = ring(region_ax, 0, step_x)
    b1, b2 = ring(region_by, 4, step_y)
    for copy in a1 + b1:
        copy.start()
    pl.when(p < 3)(up1.start)
    pl.when(p > 0)(down1.start)
    kv_steps[1].wait_recv()
    kv_steps[2].start()
    for copy in a1 + b1:
        copy.wait_recv()
    for copy in a2 + b2:
        copy.start()
    kv_steps[2].wait_recv()
    kv_steps[3].start()
    for copy in a2 + b2:
        copy.wait_recv()
    c1, c2 = ring(region_ay, 0, step_y)
    d1, d2 = ring(region_bx, 4, step_x)
    twins = {
        d: [
            remote(region_ay(d, 0, 4), region_ay(d, 0, 4), sibling),
            remote(region_bx(d, 4, 4), region_bx(d, 4, 4), sibling),
        ]
        for d in (0, 1, -1, 2)
    }
    for copy in c1 + d1 + twins[0]:
        copy.start()
    kv_steps[3].wait_recv()

    groups = 4
    for g in range(groups):
        head = lambda h: (g * 8 + h) * HD
        queries = jnp.concatenate([q_ref[:, head(h):head(h) + HD] for h in range(8)], axis=0)
        keys = kv[:, 0, :, g * HD:(g + 1) * HD].reshape(5 * 64, HD)
        values = kv[:, 1, :, g * HD:(g + 1) * HD].reshape(5 * 64, HD)
        scores = lax.dot_general(
            queries, keys, (((1,), (1,)), ((), ())), preferred_element_type=jnp.float32
        ) * (1.0 / HD**0.5)
        scores = scores.reshape(8, 64, 320) + bias_ref[...][None]
        scores = scores.reshape(512, 320)
        terms = jnp.exp(scores - jnp.max(scores, axis=-1, keepdims=True))
        probs = (terms / jnp.sum(terms, axis=-1, keepdims=True)).astype(jnp.bfloat16)
        out = jnp.dot(probs, values, preferred_element_type=jnp.float32).astype(jnp.bfloat16)
        for h in range(8):
            att[:, head(h):head(h) + HD] = out[64 * h:64 * (h + 1)]

    for copy in c1 + d1:
        copy.wait_recv()
    for copy in c2 + d2 + twins[1] + twins[-1]:
        copy.start()
    pl.when(p > 0)(up1.wait_recv)
    pl.when(p < 3)(down1.wait_recv)
    pl.when((p > 0) & (p < 3))(up2.start)
    pl.when((p > 0) & (p < 3))(down2.start)
    for copy in c2 + d2:
        copy.wait_recv()
    for copy in twins[2]:
        copy.start()
    for d in (0, 1, -1, 2):
        for copy in twins[d]:
            copy.wait_recv()

    for n in range(4):
        cols = slice(512 * n, 512 * (n + 1))
        acc = res_ref[:, cols].astype(jnp.float32)
        for t in range(8):
            acc = acc + jnp.dot(
                att[:, 512 * t:512 * (t + 1)], wbuf[t, :, cols], preferred_element_type=jnp.float32
            )
        total[:, cols] = acc
    hidden = total[...]
    hidden_ref[...] = hidden.astype(jnp.bfloat16)
    square = jnp.mean(hidden * hidden, axis=-1, keepdims=True)
    normed_ref[...] = (hidden * lax.rsqrt(square + EPSILON) * gain_ref[...]).astype(jnp.bfloat16)

    for copy in meta_copies:
        copy.wait_recv()
    pl.when(p > 1)(up2.wait_recv)
    pl.when(p < 2)(down2.wait_recv)
    for copy in kv_steps + z_copies + meta_copies + a1 + b1 + a2 + b2 + c1 + d1 + c2 + d2:
        copy.wait_send()
    for d in (0, 1, -1, 2):
        for copy in twins[d]:
            copy.wait_send()
    pl.when(p < 3)(up1.wait_send)
    pl.when(p > 0)(down1.wait_send)
    pl.when((p > 0) & (p < 3))(up2.wait_send)
    pl.when((p > 0) & (p < 3))(down2.wait_send)


def front(q, k, v, bias, res, gain, meta, wout, wg, wu, wd):
    d = res.shape[1]
    copies = 48
    return pl.pallas_call(
        front_kernel,
        out_shape=(
            jax.ShapeDtypeStruct((64, d), jnp.bfloat16),
            jax.ShapeDtypeStruct((64, d), jnp.bfloat16),
            jax.ShapeDtypeStruct((3, SUB * 96, d), jnp.bfloat16),
            jax.ShapeDtypeStruct((4, 64, 128), jnp.float32),
        ),
        in_specs=[VMEM] * 7 + [ANY] * 4,
        out_specs=(VMEM, VMEM, ANY, VMEM),
        scratch_shapes=[
            pltpu.VMEM((LINE, 512, d), jnp.bfloat16),
            pltpu.VMEM((5, 2, 64, 512), jnp.bfloat16),
            pltpu.VMEM((64, 4096), jnp.bfloat16),
            pltpu.VMEM((64, d), jnp.float32),
            pltpu.SemaphoreType.DMA((copies,)),
            pltpu.SemaphoreType.DMA((copies,)),
            pltpu.SemaphoreType.DMA((4,)),
        ],
        compiler_params=pltpu.CompilerParams(
            collective_id=0, has_side_effects=True, vmem_limit_bytes=48 * 2**20
        ),
        cost_estimate=pl.CostEstimate(flops=10**9, bytes_accessed=2 * 10**7, transcendentals=10**6),
    )(q, k, v, bias, res, gain, meta, wout, wg, wu, wd)


def back_kernel(
    normed_ref, metas_ref, wts_ref, out_ref,
    wv, pick, comb, tok, sent, got, accum, act, made, back, part, far, home,
    z_send, z_recv, h_send, h_recv, p_send, p_recv, r_send, r_recv, f_send, f_recv, o_send, o_recv,
    w_send, w_recv, local, selfs,
):
    x, y, z, c = place()
    p = z % SUB
    me = (x * Y + y) * CORES + c
    at = lambda dz: device(x, y, z + dz + Z, c)
    width = tok.shape[2]

    def plane(i):
        return device(i // (Y * CORES), (i // CORES) % Y, z, i % CORES)

    def remote(src, dst, ss, rs, peer):
        return pltpu.make_async_remote_copy(
            src_ref=src, dst_ref=dst, send_sem=ss, recv_sem=rs, device_id=peer, device_id_type=MESH
        )

    barrier = pltpu.get_barrier_semaphore()
    for d in (4, -4, 1, -1):
        pl.semaphore_signal(barrier, inc=1, device_id=at(d), device_id_type=MESH)

    def greet(o, _):
        pl.semaphore_signal(barrier, inc=1, device_id=plane((me + o) % PLANE), device_id_type=MESH)
        return 0

    lax.fori_loop(1, PLANE, greet, 0)
    pl.semaphore_wait(barrier, 4 + PLANE - 1)

    for q in range(CHUNKS):
        tok[q, 0:64] = normed_ref[:, width * q:width * (q + 1)]
    near = [
        (
            remote(tok.at[q, pl.ds(0, 64)], tok.at[q, pl.ds(64, 64)], z_send.at[q, 0], z_recv.at[q, 0], at(4)),
            remote(tok.at[q, pl.ds(0, 64)], tok.at[q, pl.ds(128, 64)], z_send.at[q, 1], z_recv.at[q, 1], at(-4)),
        )
        for q in range(CHUNKS)
    ]
    across = [
        (
            remote(tok.at[q, pl.ds(64, 32)], tok.at[q, pl.ds(192, 32)], h_send.at[q, 0], h_recv.at[q, 0], at(4)),
            remote(tok.at[q, pl.ds(160, 32)], tok.at[q, pl.ds(224, 32)], h_send.at[q, 1], h_recv.at[q, 1], at(-4)),
        )
        for q in range(CHUNKS)
    ]
    for q in range(CHUNKS):
        for copy in near[q]:
            copy.start()

    def block(ref, owner):
        return ref.at[:, pl.ds(96 * owner, 96)]

    up3 = remote(block(wts_ref, 0), block(wv, 0), w_send.at[0], w_recv.at[0], at(1))
    down3 = remote(block(wts_ref, 3), block(wv, 3), w_send.at[1], w_recv.at[1], at(-1))
    pl.when(p == 2)(up3.start)
    pl.when(p == 1)(down3.start)
    keep = [p != 3, None, None, p != 0]
    blocks = [
        pltpu.make_async_copy(block(wts_ref, m), block(wv, m), local.at[m]) for m in range(SUB)
    ]
    for m in range(SUB):
        if keep[m] is None:
            blocks[m].start()
        else:
            pl.when(keep[m])(blocks[m].start)

    for a in range(2):
        lane = lax.broadcasted_iota(jnp.int32, (PLANE, 128), 1)
        slots = jnp.where(lane < 64, metas_ref[2 * a, 0:32], metas_ref[2 * a + 1, 0:32])
        weights = jnp.where(lane < 64, metas_ref[2 * a, 32:64], metas_ref[2 * a + 1, 32:64])
        row = lax.broadcasted_iota(jnp.int32, (PLANE, 4 * CAP, 128), 1)
        column = lax.broadcasted_iota(jnp.int32, (PLANE, 4 * CAP, 128), 2)
        same = row // CAP == 2 * a + column // 64
        hit = same & (slots[:, None, :] == (row % CAP).astype(jnp.float32))
        pick[:, 128 * a:128 * (a + 1)] = (
            jnp.where(hit, 1.0, 0.0).reshape(PLANE * 4 * CAP, 128).astype(jnp.bfloat16)
        )
        comb[:, 128 * a:128 * (a + 1)] = (
            jnp.where(hit, weights[:, None, :], 0.0).reshape(PLANE * 4 * CAP, 128).astype(jnp.bfloat16)
        )

    def spread(src, dst, q, ss, rs):
        def go(o, _):
            peer = (me + o) % PLANE
            remote(
                src.at[q, rows(32 * peer, 32)], dst.at[q, rows(32 * me, 32)], ss.at[q], rs.at[q], plane(peer)
            ).start()
            return 0

        lax.fori_loop(1, PLANE, go, 0)
        dst[q, rows(32 * me, 32)] = src[q, rows(32 * me, 32)]

    def whole(src, dst, q, ss, rs):
        span = pl.ds(0, 32 * (PLANE - 1))
        return remote(src.at[q, span], dst.at[q, span], ss.at[q], rs.at[q], at(1))

    def dispatch(q):
        for copy in across[q]:
            copy.wait_recv()

        def tile(i, _):
            part_rows = pl.ds(pl.multiple_of(i * 256, 256), 256)
            sent[q, part_rows] = jnp.dot(
                pick[part_rows], tok[q], preferred_element_type=jnp.float32
            ).astype(jnp.bfloat16)
            return 0

        lax.fori_loop(0, 4, tile, 0)
        spread(sent, got, q, p_send, p_recv)

    for q in range(CHUNKS):
        for copy in near[q]:
            copy.wait_recv()
        for copy in across[q]:
            copy.start()
        if q >= 1:
            dispatch(q - 1)
    dispatch(CHUNKS - 1)

    for m in range(SUB):
        if keep[m] is None:
            blocks[m].wait()
        else:
            pl.when(keep[m])(blocks[m].wait)
    pl.when(p == 3)(up3.wait_recv)
    pl.when(p == 0)(down3.wait_recv)
    hidden_units = SUB * 96
    transposed = (((1,), (1,)), ((), ()))
    for q in range(CHUNKS):
        whole(sent, got, q, p_send, p_recv).wait_recv()
        cols = slice(width * q, width * (q + 1))

        def tile(i, _, q=q, cols=cols):
            part_rows = pl.ds(pl.multiple_of(i * 256, 256), 256)
            for m in range(2):
                value = lax.dot_general(
                    got[q, part_rows], wv[m, :, cols], transposed, preferred_element_type=jnp.float32
                )
                if q == 0:
                    accum[m, part_rows] = value
                else:
                    accum[m, part_rows] += value
            return 0

        lax.fori_loop(0, 4, tile, 0)

    def activate(i, _):
        part_rows = pl.ds(pl.multiple_of(i * 256, 256), 256)
        gate = accum[0, part_rows]
        act[part_rows] = (gate / (1.0 + jnp.exp(-gate)) * accum[1, part_rows]).astype(jnp.bfloat16)
        return 0

    lax.fori_loop(0, 4, activate, 0)

    for q in range(CHUNKS):
        cols = slice(width * q, width * (q + 1))

        def tile(i, _, q=q, cols=cols):
            part_rows = pl.ds(pl.multiple_of(i * 256, 256), 256)
            made[q, part_rows] = jnp.dot(
                act[part_rows], wv[2, :, cols], preferred_element_type=jnp.float32
            ).astype(jnp.bfloat16)
            return 0

        lax.fori_loop(0, 4, tile, 0)
        spread(made, back, q, r_send, r_recv)

    def half_copies(q):
        return (
            remote(far.at[q, 0, pl.ds(0, 32)], home.at[q, 0, pl.ds(0, 32)], f_send.at[q, 0], f_recv.at[q, 0], at(4)),
            remote(far.at[q, 0, pl.ds(32, 32)], home.at[q, 0, pl.ds(32, 32)], f_send.at[q, 1], f_recv.at[q, 1], at(-4)),
        )

    def home_copies(q):
        return (
            remote(far.at[q, 1], home.at[q, 1], o_send.at[q, 0], o_recv.at[q, 0], at(-4)),
            remote(far.at[q, 2], home.at[q, 2], o_send.at[q, 1], o_recv.at[q, 1], at(4)),
        )

    def combine(q):
        whole(made, back, q, r_send, r_recv).wait_recv()
        part[q] = lax.dot_general(
            comb[...], back[q], (((0,), (0,)), ((), ())), preferred_element_type=jnp.float32
        )
        far[q, 0] = part[q, 192:256].astype(jnp.bfloat16)
        for copy in half_copies(q):
            copy.start()

    def relay(q):
        for copy in half_copies(q):
            copy.wait_recv()
        ahead, behind = part[q, 128:192], part[q, 64:128]
        far[q, 2, 0:32] = (ahead[0:32] + home[q, 0, 0:32].astype(jnp.float32)).astype(jnp.bfloat16)
        far[q, 2, 32:64] = ahead[32:64].astype(jnp.bfloat16)
        far[q, 1, 0:32] = behind[0:32].astype(jnp.bfloat16)
        far[q, 1, 32:64] = (behind[32:64] + home[q, 0, 32:64].astype(jnp.float32)).astype(jnp.bfloat16)
        for copy in home_copies(q):
            copy.start()

    def finish(q):
        for copy in home_copies(q):
            copy.wait_recv()
        total = part[q, 0:64] + home[q, 1].astype(jnp.float32) + home[q, 2].astype(jnp.float32)
        out_ref[:, width * q:width * (q + 1)] = total.astype(jnp.bfloat16)

    for step in range(CHUNKS + 2):
        if step < CHUNKS:
            combine(step)
        if 0 <= step - 1 < CHUNKS:
            relay(step - 1)
        if 0 <= step - 2 < CHUNKS:
            finish(step - 2)

    for q in range(CHUNKS):
        for copy in near[q] + across[q] + half_copies(q) + home_copies(q):
            copy.wait_send()
        whole(sent, got, q, p_send, p_recv).wait_send()
        whole(made, back, q, r_send, r_recv).wait_send()
    pl.when(p == 2)(up3.wait_send)
    pl.when(p == 1)(down3.wait_send)


def behind(normed, metas, wts):
    d = normed.shape[1]
    width = d // CHUNKS
    slots = PLANE * 4 * CAP
    units = SUB * 96
    dma = lambda *shape: pltpu.SemaphoreType.DMA(shape)
    return pl.pallas_call(
        back_kernel,
        out_shape=jax.ShapeDtypeStruct((64, d), jnp.bfloat16),
        in_specs=[VMEM, VMEM, ANY],
        out_specs=VMEM,
        scratch_shapes=[
            pltpu.VMEM((3, units, d), jnp.bfloat16),
            pltpu.VMEM((slots, 256), jnp.bfloat16),
            pltpu.VMEM((slots, 256), jnp.bfloat16),
            pltpu.VMEM((CHUNKS, 256, width), jnp.bfloat16),
            pltpu.VMEM((CHUNKS, slots, width), jnp.bfloat16),
            pltpu.VMEM((CHUNKS, slots, width), jnp.bfloat16),
            pltpu.VMEM((2, slots, units), jnp.float32),
            pltpu.VMEM((slots, units), jnp.bfloat16),
            pltpu.VMEM((CHUNKS, slots, width), jnp.bfloat16),
            pltpu.VMEM((CHUNKS, slots, width), jnp.bfloat16),
            pltpu.VMEM((CHUNKS, 256, width), jnp.float32),
            pltpu.VMEM((CHUNKS, 3, 64, width), jnp.bfloat16),
            pltpu.VMEM((CHUNKS, 3, 64, width), jnp.bfloat16),
            dma(CHUNKS, 2), dma(CHUNKS, 2), dma(CHUNKS, 2), dma(CHUNKS, 2),
            dma(CHUNKS), dma(CHUNKS), dma(CHUNKS), dma(CHUNKS),
            dma(CHUNKS, 2), dma(CHUNKS, 2), dma(CHUNKS, 2), dma(CHUNKS, 2),
            dma(2), dma(2), dma(SUB), dma(2),
        ],
        compiler_params=pltpu.CompilerParams(
            collective_id=1, has_side_effects=True, vmem_limit_bytes=52 * 2**20
        ),
        cost_estimate=pl.CostEstimate(flops=6 * 10**9, bytes_accessed=10**7, transcendentals=10**6),
    )(normed, metas, wts)


def routing(ids, keep, logits):
    experts = logits.shape[1]
    hit = ids[:, :, None] == jnp.arange(experts, dtype=jnp.int32)
    named = jnp.any(hit, axis=1)
    kept = jnp.any(hit & (keep[:, :, None] == 1), axis=1)
    tokens = ids.shape[0]
    earlier = jnp.tril(jnp.ones((tokens, tokens), jnp.bfloat16), -1)
    before = jnp.dot(earlier, kept.astype(jnp.bfloat16), preferred_element_type=jnp.float32)
    slot = jnp.where(kept, before, -1.0)
    chosen = jnp.where(named, logits, -jnp.inf)
    terms = jnp.exp(chosen - jnp.max(chosen, axis=-1, keepdims=True))
    probs = terms / jnp.sum(terms, axis=-1, keepdims=True)
    weight = jnp.where(kept, probs, 0.0)
    both = jnp.stack([slot, weight])
    both = jnp.transpose(both, (0, 2, 1)).reshape(2, X, 2, Y * CORES, tokens)
    both = jnp.transpose(both, (2, 0, 1, 3, 4)).reshape(2, 2 * PLANE, tokens)
    return jnp.concatenate([both, both], axis=-1)


def shards(
    queries, key_heads, value_heads, doc_ids, residual, w_out, norm_gain, router_logits, expert_ids, keep_mask,
    w_gate, w_up, w_down,
):
    s = lax.axis_index("seq")
    doc = jnp.pad(doc_ids[0], (256, 0), constant_values=-1)
    span = lax.dynamic_slice(doc, (64 * s,), (320,))
    causal = jnp.arange(320)[None, :] <= 256 + jnp.arange(64)[:, None]
    bias = jnp.where(causal & (span[None, :] == span[256:, None]), 0.0, NEG).astype(jnp.float32)
    meta = routing(expert_ids[0], keep_mask[0], router_logits[0])
    hidden, normed, wts, metas = front(
        queries[0], key_heads[0], value_heads[0], bias, residual[0], norm_gain[None], meta, w_out,
        w_gate[0], w_up[0], w_down[0],
    )
    return hidden[None], behind(normed, metas, wts)[None]


def solution(mesh):
    split = P("exp", "seq", None)
    return jax.shard_map(
        shards,
        mesh=mesh,
        in_specs=(split, split, split, P("exp", None), split, P("seq", None), P()) + (split,) * 6,
        out_specs=(split, split),
        check_vma=False,
    )
```

```python
import jax
import jax.numpy as jnp
from jax import lax
from jax.experimental import pallas as pl
from jax.experimental.pallas import tpu as pltpu
from jax.sharding import PartitionSpec as P

MESH = pl.DeviceIdType.MESH
HD = 128
CAP = 8
X, Y, Z, LINE, CORES = 4, 4, 16, 8, 2
PLANE = X * Y * CORES
SUB = 4
CHUNKS = 4
EPSILON = 1e-06
NEG = -1e30
ANY = pl.BlockSpec(memory_space=pl.ANY)
VMEM = pl.BlockSpec(memory_space=pltpu.VMEM)
Z_OFFSETS = (1, -1, 2, -2, 3, -3, 4)


def place():
    s = lax.axis_index("seq")
    e = lax.axis_index("exp")
    c = e % 2
    y = (e // 2) % Y
    zh = (e // (2 * Y)) % 2
    x = e // (4 * Y)
    return x, y, zh * LINE + s, c


def device(x, y, z, c):
    x, y, z = x % X, y % Y, z % Z
    return {"seq": z % LINE, "exp": ((x * 2 + z // LINE) * Y + y) * 2 + c}


def rows(start, count):
    return pl.ds(pl.multiple_of(start, 16), count)


def layer_kernel(
    q_hbm, k_hbm, v_hbm, span_hbm, res_hbm, gain_hbm, logits_hbm, ids_hbm, keep_hbm, wout_ref, wg_ref, wu_ref, wd_ref,
    hidden_ref, out_ref,
    q_ref, kv, span_ref, res_ref, gain_ref, logits_ref, ids_ref, keep_ref, meta, metas,
    wbuf, att, total, wv, pick, comb, tok, sent, got, accum, act, made, back, part, far, home,
    send, recv, local,
    z_send, z_recv, h_send, h_recv, p_send, p_recv, r_send, r_recv, f_send, f_recv, o_send, o_recv,
):
    x, y, z, c = place()
    s = z % LINE
    zh = z // LINE
    p = z % SUB
    me = (x * Y + y) * CORES + c
    width = tok.shape[2]

    def at(dx=0, dy=0, dz=0):
        return device(x + dx + X, y + dy + Y, z + dz + Z, c)

    def partner(o):
        dx = o % X
        px = (x + dx) % X
        py = (y + o // (X * CORES) + dx) % Y
        pc = (c + o // X) % CORES
        return (px * Y + py) * CORES + pc, device(px, py, z, pc)

    sibling = device(x, y, z, 1 - c)
    counter = [0]

    def remote(src, dst, peer):
        i = counter[0]
        counter[0] += 1
        return copy_to(src, dst, send.at[i], recv.at[i], peer)

    def copy_to(src, dst, ss, rs, peer):
        return pltpu.make_async_remote_copy(
            src_ref=src, dst_ref=dst, send_sem=ss, recv_sem=rs, device_id=peer, device_id_type=MESH
        )

    def block(owner):
        return wv.at[:, rows(96 * ((owner + SUB) % SUB), 96)]

    ja = (y * 2 + c) * X + x
    jb = (x * 2 + c) * Y + y
    mine = jnp.where(s < 4, ja, jb) * 16
    piece = wbuf.at[s, rows(mine, 16)]
    moves = [
        (k_hbm, kv.at[4, 0]), (v_hbm, kv.at[4, 1]), (wout_ref.at[rows(mine, 16)], piece),
        (ids_hbm, ids_ref), (keep_hbm, keep_ref), (logits_hbm, logits_ref), (span_hbm, span_ref),
        (wg_ref, wv.at[0, rows(96 * p, 96)]), (wu_ref, wv.at[1, rows(96 * p, 96)]),
        (wd_ref, wv.at[2, rows(96 * p, 96)]),
        (q_hbm, q_ref), (res_hbm, res_ref), (gain_hbm, gain_ref),
    ]
    loads = [pltpu.make_async_copy(src, dst, local.at[i]) for i, (src, dst) in enumerate(moves)]
    for load in loads:
        load.start()

    barrier = pltpu.get_barrier_semaphore()
    for d in (1, -1, 2, -2, 3, -3, 4, -4, 8):
        pl.semaphore_signal(barrier, inc=1, device_id=at(dz=d), device_id_type=MESH)

    def greet(o, _):
        pl.semaphore_signal(barrier, inc=1, device_id=partner(o)[1], device_id_type=MESH)
        return 0

    lax.fori_loop(1, PLANE, greet, 0)
    pl.semaphore_wait(barrier, 9 + PLANE - 1)

    kv_steps = [remote(kv.at[4 - d], kv.at[3 - d], at(dz=1)) for d in range(4)]
    z_copies = [remote(piece, piece, at(dz=d)) for d in Z_OFFSETS]
    for load in loads[:3]:
        load.wait()
    for copy in z_copies:
        copy.start()
    kv_steps[0].start()

    for load in loads[3:7]:
        load.wait()
    experts = logits_ref.shape[1]
    expert = lax.broadcasted_iota(jnp.int32, (experts, 64), 0)
    named = expert == ids_ref[0:1, :]
    kept = named & (keep_ref[0:1, :] == 1)
    for k in range(1, ids_ref.shape[0]):
        hit = expert == ids_ref[k:k + 1, :]
        named = named | hit
        kept = kept | (hit & (keep_ref[k:k + 1, :] == 1))
    earlier = lax.broadcasted_iota(jnp.int32, (64, 64), 0) < lax.broadcasted_iota(jnp.int32, (64, 64), 1)
    before = jnp.dot(
        jnp.where(kept, 1.0, 0.0).astype(jnp.bfloat16),
        jnp.where(earlier, 1.0, 0.0).astype(jnp.bfloat16),
        preferred_element_type=jnp.float32,
    )
    slot = jnp.where(kept, before, -1.0)
    chosen = jnp.where(named, logits_ref[...], -jnp.inf)
    terms = jnp.exp(chosen - jnp.max(chosen, axis=0, keepdims=True))
    weight = jnp.where(kept, terms / jnp.sum(terms, axis=0, keepdims=True), 0.0)
    slot = jnp.concatenate([slot, slot], axis=1)
    weight = jnp.concatenate([weight, weight], axis=1)
    group = Y * CORES
    for half in range(2):
        for i in range(X):
            chunk = slice(group * (2 * i + half), group * (2 * i + half + 1))
            meta[half, group * i:group * (i + 1)] = slot[chunk]
            meta[half, PLANE + group * i:PLANE + group * (i + 1)] = weight[chunk]
    metas[0] = meta[zh]
    meta_copies = [
        remote(meta.at[1 - zh], metas.at[3], at(dz=8)),
        remote(meta.at[((z + 4) % Z) // LINE], metas.at[1], at(dz=4)),
        remote(meta.at[((z + 12) % Z) // LINE], metas.at[2], at(dz=-4)),
    ]
    for copy in meta_copies:
        copy.start()

    kv_steps[0].wait_recv()
    kv_steps[1].start()
    for copy in z_copies:
        copy.wait_recv()

    up1 = remote(block(p), block(p), at(dz=1))
    down1 = remote(block(p), block(p), at(dz=-1))
    up2 = remote(block(p - 1), block(p - 1), at(dz=1))
    down2 = remote(block(p + 1), block(p + 1), at(dz=-1))
    up3 = remote(block(0), block(0), at(dz=1))
    down3 = remote(block(3), block(3), at(dz=-1))

    def ring(region, lo, step):
        first = [remote(region(0, lo, 4), region(0, lo, 4), step(d)) for d in (1, -1)]
        second = [
            remote(region(-1, lo, 2), region(-1, lo, 2), step(1)),
            remote(region(1, lo + 2, 2), region(1, lo + 2, 2), step(-1)),
        ]
        return first, second

    def region_ax(d, lo, n):
        return wbuf.at[pl.ds(lo, n), rows(16 * ((y * 2 + c) * X + (x + d + X) % X), 16)]

    def region_by(d, lo, n):
        return wbuf.at[pl.ds(lo, n), rows(16 * ((x * 2 + c) * Y + (y + d + Y) % Y), 16)]

    def region_ay(d, lo, n):
        return wbuf.at[pl.ds(lo, n), rows(64 * (((y + d + Y) % Y) * 2 + c), 64)]

    def region_bx(d, lo, n):
        return wbuf.at[pl.ds(lo, n), rows(64 * (((x + d + X) % X) * 2 + c), 64)]

    step_x = lambda d: at(dx=d)
    step_y = lambda d: at(dy=d)
    a1, a2 = ring(region_ax, 0, step_x)
    b1, b2 = ring(region_by, 4, step_y)
    for copy in a1 + b1:
        copy.start()
    for load in loads[7:10]:
        load.wait()
    pl.when(p < 3)(up1.start)
    pl.when(p > 0)(down1.start)
    kv_steps[1].wait_recv()
    kv_steps[2].start()
    for copy in a1 + b1:
        copy.wait_recv()
    for copy in a2 + b2:
        copy.start()
    kv_steps[2].wait_recv()
    kv_steps[3].start()
    for copy in a2 + b2:
        copy.wait_recv()
    c1, c2 = ring(region_ay, 0, step_y)
    d1, d2 = ring(region_bx, 4, step_x)
    twins = {
        d: [
            remote(region_ay(d, 0, 4), region_ay(d, 0, 4), sibling),
            remote(region_bx(d, 4, 4), region_bx(d, 4, 4), sibling),
        ]
        for d in (0, 1, -1, 2)
    }
    for copy in c1 + d1 + twins[0]:
        copy.start()

    for copy in meta_copies:
        copy.wait_recv()
    for a in range(2):
        lane = lax.broadcasted_iota(jnp.int32, (PLANE, 128), 1)
        slots = jnp.where(lane < 64, metas[2 * a, 0:PLANE], metas[2 * a + 1, 0:PLANE])
        weights = jnp.where(lane < 64, metas[2 * a, PLANE:], metas[2 * a + 1, PLANE:])
        row = lax.broadcasted_iota(jnp.int32, (PLANE, 4 * CAP, 128), 1)
        column = lax.broadcasted_iota(jnp.int32, (PLANE, 4 * CAP, 128), 2)
        same = row // CAP == 2 * a + column // 64
        hit = same & (slots[:, None, :] == (row % CAP).astype(jnp.float32))
        pick[:, 128 * a:128 * (a + 1)] = (
            jnp.where(hit, 1.0, 0.0).reshape(PLANE * 4 * CAP, 128).astype(jnp.bfloat16)
        )
        comb[:, 128 * a:128 * (a + 1)] = (
            jnp.where(hit, weights[:, None, :], 0.0).reshape(PLANE * 4 * CAP, 128).astype(jnp.bfloat16)
        )

    docs = lax.broadcasted_iota(jnp.int32, (8, 320), 0)
    key_doc = jnp.where(docs == span_ref[...], 1.0, 0.0).astype(jnp.bfloat16)
    same_doc = lax.dot_general(
        key_doc[:, 256:320], key_doc, (((0,), (0,)), ((), ())), preferred_element_type=jnp.float32
    )
    key_at = lax.broadcasted_iota(jnp.int32, (64, 320), 1)
    query_at = lax.broadcasted_iota(jnp.int32, (64, 320), 0)
    bias = jnp.where((key_at <= query_at + 256) & (same_doc > 0.5), 0.0, NEG)
    loads[10].wait()
    kv_steps[3].wait_recv()
    for g in range(4):
        head = lambda h: (g * 8 + h) * HD
        queries = jnp.concatenate([q_ref[:, head(h):head(h) + HD] for h in range(8)], axis=0)
        keys = kv[:, 0, :, g * HD:(g + 1) * HD].reshape(5 * 64, HD)
        values = kv[:, 1, :, g * HD:(g + 1) * HD].reshape(5 * 64, HD)
        scores = lax.dot_general(
            queries, keys, (((1,), (1,)), ((), ())), preferred_element_type=jnp.float32
        ) * (1.0 / HD**0.5)
        scores = (scores.reshape(8, 64, 320) + bias[None]).reshape(512, 320)
        terms = jnp.exp(scores - jnp.max(scores, axis=-1, keepdims=True))
        probs = (terms / jnp.sum(terms, axis=-1, keepdims=True)).astype(jnp.bfloat16)
        out = jnp.dot(probs, values, preferred_element_type=jnp.float32).astype(jnp.bfloat16)
        for h in range(8):
            att[:, head(h):head(h) + HD] = out[64 * h:64 * (h + 1)]

    pl.when(p > 0)(up1.wait_recv)
    pl.when(p < 3)(down1.wait_recv)
    pl.when((p > 0) & (p < 3))(up2.start)
    pl.when((p > 0) & (p < 3))(down2.start)
    for copy in c1 + d1:
        copy.wait_recv()
    for copy in c2 + d2 + twins[1] + twins[-1]:
        copy.start()
    for copy in c2 + d2:
        copy.wait_recv()
    for copy in twins[2]:
        copy.start()
    pl.when(p > 1)(up2.wait_recv)
    pl.when(p < 2)(down2.wait_recv)
    pl.when(p == 2)(up3.start)
    pl.when(p == 1)(down3.start)
    for d in (0, 1, -1, 2):
        for copy in twins[d]:
            copy.wait_recv()

    for load in loads[11:]:
        load.wait()
    for n in range(4):
        cols = slice(512 * n, 512 * (n + 1))
        acc = res_ref[:, cols].astype(jnp.float32)
        for t in range(8):
            acc = acc + jnp.dot(
                att[:, 512 * t:512 * (t + 1)], wbuf[t, :, cols], preferred_element_type=jnp.float32
            )
        total[:, cols] = acc
    hidden = total[...]
    square = jnp.mean(hidden * hidden, axis=-1, keepdims=True)
    normed = (hidden * lax.rsqrt(square + EPSILON) * gain_ref[...]).astype(jnp.bfloat16)
    for q in range(CHUNKS):
        tok[q, 0:64] = normed[:, width * q:width * (q + 1)]

    near = [
        (
            copy_to(tok.at[q, pl.ds(0, 64)], tok.at[q, pl.ds(64, 64)], z_send.at[q, 0], z_recv.at[q, 0], at(dz=4)),
            copy_to(tok.at[q, pl.ds(0, 64)], tok.at[q, pl.ds(128, 64)], z_send.at[q, 1], z_recv.at[q, 1], at(dz=-4)),
        )
        for q in range(CHUNKS)
    ]
    across = [
        (
            copy_to(tok.at[q, pl.ds(64, 32)], tok.at[q, pl.ds(192, 32)], h_send.at[q, 0], h_recv.at[q, 0], at(dz=4)),
            copy_to(tok.at[q, pl.ds(160, 32)], tok.at[q, pl.ds(224, 32)], h_send.at[q, 1], h_recv.at[q, 1], at(dz=-4)),
        )
        for q in range(CHUNKS)
    ]
    for q in range(CHUNKS):
        for copy in near[q]:
            copy.start()
    hidden_ref[...] = hidden.astype(jnp.bfloat16)

    def spread(src, dst, q, ss, rs):
        def go(o, _):
            peer, where = partner(o)
            copy_to(
                src.at[q, rows(32 * peer, 32)], dst.at[q, rows(32 * me, 32)], ss.at[q], rs.at[q], where
            ).start()
            return 0

        lax.fori_loop(1, PLANE, go, 0)
        dst[q, rows(32 * me, 32)] = src[q, rows(32 * me, 32)]

    def whole(src, dst, q, ss, rs):
        every = pl.ds(0, 32 * (PLANE - 1))
        return copy_to(src.at[q, every], dst.at[q, every], ss.at[q], rs.at[q], at(dz=1))

    def dispatch(q):
        for copy in across[q]:
            copy.wait_recv()

        def tile(i, _):
            part_rows = pl.ds(pl.multiple_of(i * 256, 256), 256)
            sent[q, part_rows] = jnp.dot(
                pick[part_rows], tok[q], preferred_element_type=jnp.float32
            ).astype(jnp.bfloat16)
            return 0

        lax.fori_loop(0, 4, tile, 0)
        spread(sent, got, q, p_send, p_recv)

    for q in range(CHUNKS):
        for copy in near[q]:
            copy.wait_recv()
        for copy in across[q]:
            copy.start()
        if q >= 1:
            dispatch(q - 1)
    dispatch(CHUNKS - 1)

    pl.when(p == 3)(up3.wait_recv)
    pl.when(p == 0)(down3.wait_recv)
    transposed = (((1,), (1,)), ((), ()))
    for q in range(CHUNKS):
        whole(sent, got, q, p_send, p_recv).wait_recv()
        cols = slice(width * q, width * (q + 1))

        def tile(i, _, q=q, cols=cols):
            part_rows = pl.ds(pl.multiple_of(i * 256, 256), 256)
            for m in range(2):
                value = lax.dot_general(
                    got[q, part_rows], wv[m, :, cols], transposed, preferred_element_type=jnp.float32
                )
                if q == 0:
                    accum[m, part_rows] = value
                else:
                    accum[m, part_rows] += value
            return 0

        lax.fori_loop(0, 4, tile, 0)

    def activate(i, _):
        part_rows = pl.ds(pl.multiple_of(i * 256, 256), 256)
        gate = accum[0, part_rows]
        act[part_rows] = (gate / (1.0 + jnp.exp(-gate)) * accum[1, part_rows]).astype(jnp.bfloat16)
        return 0

    lax.fori_loop(0, 4, activate, 0)

    for q in range(CHUNKS):
        cols = slice(width * q, width * (q + 1))

        def tile(i, _, q=q, cols=cols):
            part_rows = pl.ds(pl.multiple_of(i * 256, 256), 256)
            made[q, part_rows] = jnp.dot(
                act[part_rows], wv[2, :, cols], preferred_element_type=jnp.float32
            ).astype(jnp.bfloat16)
            return 0

        lax.fori_loop(0, 4, tile, 0)
        spread(made, back, q, r_send, r_recv)

    def half_copies(q):
        return (
            copy_to(far.at[q, 0, pl.ds(0, 32)], home.at[q, 0, pl.ds(0, 32)], f_send.at[q, 0], f_recv.at[q, 0], at(dz=4)),
            copy_to(far.at[q, 0, pl.ds(32, 32)], home.at[q, 0, pl.ds(32, 32)], f_send.at[q, 1], f_recv.at[q, 1], at(dz=-4)),
        )

    def home_copies(q):
        return (
            copy_to(far.at[q, 1], home.at[q, 1], o_send.at[q, 0], o_recv.at[q, 0], at(dz=-4)),
            copy_to(far.at[q, 2], home.at[q, 2], o_send.at[q, 1], o_recv.at[q, 1], at(dz=4)),
        )

    def combine(q):
        whole(made, back, q, r_send, r_recv).wait_recv()
        part[q] = lax.dot_general(
            comb[...], back[q], (((0,), (0,)), ((), ())), preferred_element_type=jnp.float32
        )
        far[q, 0] = part[q, 192:256].astype(jnp.bfloat16)
        for copy in half_copies(q):
            copy.start()

    def relay(q):
        for copy in half_copies(q):
            copy.wait_recv()
        ahead, behind = part[q, 128:192], part[q, 64:128]
        far[q, 2, 0:32] = (ahead[0:32] + home[q, 0, 0:32].astype(jnp.float32)).astype(jnp.bfloat16)
        far[q, 2, 32:64] = ahead[32:64].astype(jnp.bfloat16)
        far[q, 1, 0:32] = behind[0:32].astype(jnp.bfloat16)
        far[q, 1, 32:64] = (behind[32:64] + home[q, 0, 32:64].astype(jnp.float32)).astype(jnp.bfloat16)
        for copy in home_copies(q):
            copy.start()

    def finish(q):
        for copy in home_copies(q):
            copy.wait_recv()
        total = part[q, 0:64] + home[q, 1].astype(jnp.float32) + home[q, 2].astype(jnp.float32)
        out_ref[:, width * q:width * (q + 1)] = total.astype(jnp.bfloat16)

    for step in range(CHUNKS + 2):
        if step < CHUNKS:
            combine(step)
        if 0 <= step - 1 < CHUNKS:
            relay(step - 1)
        if 0 <= step - 2 < CHUNKS:
            finish(step - 2)

    for q in range(CHUNKS):
        for copy in near[q] + across[q] + half_copies(q) + home_copies(q):
            copy.wait_send()
        whole(sent, got, q, p_send, p_recv).wait_send()
        whole(made, back, q, r_send, r_recv).wait_send()
    for copy in kv_steps + z_copies + meta_copies + a1 + b1 + a2 + b2 + c1 + d1 + c2 + d2:
        copy.wait_send()
    for d in (0, 1, -1, 2):
        for copy in twins[d]:
            copy.wait_send()
    pl.when(p < 3)(up1.wait_send)
    pl.when(p > 0)(down1.wait_send)
    pl.when((p > 0) & (p < 3))(up2.wait_send)
    pl.when((p > 0) & (p < 3))(down2.wait_send)
    pl.when(p == 2)(up3.wait_send)
    pl.when(p == 1)(down3.wait_send)


def layer(*args):
    d = args[4].shape[1]
    width = d // CHUNKS
    slots = PLANE * 4 * CAP
    units = SUB * 96
    dma = lambda *shape: pltpu.SemaphoreType.DMA(shape)
    half = lambda *shape: pltpu.VMEM(shape, jnp.bfloat16)
    full = lambda *shape: pltpu.VMEM(shape, jnp.float32)
    return pl.pallas_call(
        layer_kernel,
        out_shape=(jax.ShapeDtypeStruct((64, d), jnp.bfloat16), jax.ShapeDtypeStruct((64, d), jnp.bfloat16)),
        in_specs=[ANY] * len(args),
        out_specs=(VMEM, VMEM),
        scratch_shapes=[
            half(64, 4096), half(5, 2, 64, 512), pltpu.VMEM((1, 320), jnp.int32), half(64, d), full(1, d),
            full(64, 64), pltpu.VMEM((8, 64), jnp.int32), pltpu.VMEM((8, 64), jnp.int32),
            full(2, 64, 128), full(4, 64, 128),
            half(LINE, 512, d), half(64, 4096), full(64, d), half(3, units, d),
            half(slots, 256), half(slots, 256), half(CHUNKS, 256, width),
            half(CHUNKS, slots, width), half(CHUNKS, slots, width),
            full(2, slots, units), half(slots, units),
            half(CHUNKS, slots, width), half(CHUNKS, slots, width),
            full(CHUNKS, 256, width), half(CHUNKS, 3, 64, width), half(CHUNKS, 3, 64, width),
            dma(48), dma(48), dma(13),
            dma(CHUNKS, 2), dma(CHUNKS, 2), dma(CHUNKS, 2), dma(CHUNKS, 2),
            dma(CHUNKS), dma(CHUNKS), dma(CHUNKS), dma(CHUNKS),
            dma(CHUNKS, 2), dma(CHUNKS, 2), dma(CHUNKS, 2), dma(CHUNKS, 2),
        ],
        compiler_params=pltpu.CompilerParams(
            collective_id=0, has_side_effects=True, vmem_limit_bytes=60 * 2**20
        ),
        cost_estimate=pl.CostEstimate(flops=7 * 10**9, bytes_accessed=3 * 10**7, transcendentals=10**6),
    )(*args)


def shards(
    queries, key_heads, value_heads, doc_ids, residual, w_out, norm_gain, router_logits, expert_ids, keep_mask,
    w_gate, w_up, w_down,
):
    s = lax.axis_index("seq")
    doc = jnp.pad(doc_ids[0], (256, 0), constant_values=-1)
    span = lax.dynamic_slice(doc, (64 * s,), (320,))[None]
    hidden, out = layer(
        queries[0], key_heads[0], value_heads[0], span, residual[0], norm_gain[None], router_logits[0].T,
        expert_ids[0].T, keep_mask[0].T, w_out, w_gate[0], w_up[0], w_down[0],
    )
    return hidden[None], out[None]


def solution(mesh):
    split = P("exp", "seq", None)
    return jax.shard_map(
        shards,
        mesh=mesh,
        in_specs=(split, split, split, P("exp", None), split, P("seq", None), P()) + (split,) * 6,
        out_specs=(split, split),
        check_vma=False,
    )
```

```python
import jax
import jax.numpy as jnp
from jax import lax
from jax.experimental import pallas as pl
from jax.experimental.pallas import tpu as pltpu
from jax.sharding import PartitionSpec as P

MESH = pl.DeviceIdType.MESH
HD = 128
CAP = 8
X, Y, Z, LINE, CORES = 4, 4, 16, 8, 2
PLANE = X * Y * CORES
SUB = 4
CHUNKS = 4
EPSILON = 1e-06
NEG = -1e30
ANY = pl.BlockSpec(memory_space=pl.ANY)
VMEM = pl.BlockSpec(memory_space=pltpu.VMEM)
Z_OFFSETS = (1, -1, 2, -2, 3, -3, 4)


def place():
    s = lax.axis_index("seq")
    e = lax.axis_index("exp")
    c = e % 2
    y = (e // 2) % Y
    zh = (e // (2 * Y)) % 2
    x = e // (4 * Y)
    return x, y, zh * LINE + s, c


def device(x, y, z, c):
    x, y, z = x % X, y % Y, z % Z
    return {"seq": z % LINE, "exp": ((x * 2 + z // LINE) * Y + y) * 2 + c}


def rows(start, count):
    return pl.ds(pl.multiple_of(start, 16), count)


def layer_kernel(
    q_hbm, k_hbm, v_hbm, span_hbm, res_hbm, gain_hbm, logits_hbm, ids_hbm, keep_hbm, wout_ref, wg_ref, wu_ref, wd_ref,
    hidden_ref, out_ref,
    q_ref, kv, span_ref, res_ref, gain_ref, logits_ref, ids_ref, keep_ref, meta, metas,
    wbuf, att, total, wv, pick, comb, tok, sent, got, accum, act, made, back, part, far, home,
    send, recv, local,
    z_send, z_recv, h_send, h_recv, p_send, p_recv, r_send, r_recv, f_send, f_recv, o_send, o_recv,
):
    x, y, z, c = place()
    s = z % LINE
    zh = z // LINE
    p = z % SUB
    me = (x * Y + y) * CORES + c
    width = tok.shape[2]

    def at(dx=0, dy=0, dz=0):
        return device(x + dx + X, y + dy + Y, z + dz + Z, c)

    def partner(o):
        dx = o % X
        px = (x + dx) % X
        py = (y + o // (X * CORES) + dx) % Y
        pc = (c + o // X) % CORES
        return (px * Y + py) * CORES + pc, device(px, py, z, pc)

    sibling = device(x, y, z, 1 - c)
    counter = [0]

    def remote(src, dst, peer):
        i = counter[0]
        counter[0] += 1
        return copy_to(src, dst, send.at[i], recv.at[i], peer)

    def copy_to(src, dst, ss, rs, peer):
        return pltpu.make_async_remote_copy(
            src_ref=src, dst_ref=dst, send_sem=ss, recv_sem=rs, device_id=peer, device_id_type=MESH
        )

    def block(owner):
        return wv.at[:, rows(96 * ((owner + SUB) % SUB), 96)]

    ja = (y * 2 + c) * X + x
    jb = (x * 2 + c) * Y + y
    mine = jnp.where(s < 4, ja, jb) * 16
    piece = wbuf.at[s, rows(mine, 16)]
    moves = [
        (k_hbm, kv.at[4, 0]), (v_hbm, kv.at[4, 1]), (wout_ref.at[rows(mine, 16)], piece),
        (ids_hbm, ids_ref), (keep_hbm, keep_ref), (logits_hbm, logits_ref), (span_hbm, span_ref),
        (wg_ref, wv.at[0, rows(96 * p, 96)]), (wu_ref, wv.at[1, rows(96 * p, 96)]),
        (wd_ref, wv.at[2, rows(96 * p, 96)]),
        (q_hbm, q_ref), (res_hbm, res_ref), (gain_hbm, gain_ref),
    ]
    loads = [pltpu.make_async_copy(src, dst, local.at[i]) for i, (src, dst) in enumerate(moves)]
    for load in loads:
        load.start()

    barrier = pltpu.get_barrier_semaphore()
    for d in (1, -1, 2, -2, 3, -3, 4, -4, 8):
        pl.semaphore_signal(barrier, inc=1, device_id=at(dz=d), device_id_type=MESH)

    def greet(o, _):
        pl.semaphore_signal(barrier, inc=1, device_id=partner(o)[1], device_id_type=MESH)
        return 0

    lax.fori_loop(1, PLANE, greet, 0)
    pl.semaphore_wait(barrier, 9 + PLANE - 1)

    kv_steps = [remote(kv.at[4 - d], kv.at[3 - d], at(dz=1)) for d in range(4)]
    z_copies = [remote(piece, piece, at(dz=d)) for d in Z_OFFSETS]
    for load in loads[:3]:
        load.wait()
    for copy in z_copies:
        copy.start()
    kv_steps[0].start()

    for load in loads[3:7]:
        load.wait()
    experts = logits_ref.shape[1]
    expert = lax.broadcasted_iota(jnp.int32, (experts, 64), 0)
    named = expert == ids_ref[0:1, :]
    kept = named & (keep_ref[0:1, :] == 1)
    for k in range(1, ids_ref.shape[0]):
        hit = expert == ids_ref[k:k + 1, :]
        named = named | hit
        kept = kept | (hit & (keep_ref[k:k + 1, :] == 1))
    earlier = lax.broadcasted_iota(jnp.int32, (64, 64), 0) < lax.broadcasted_iota(jnp.int32, (64, 64), 1)
    before = jnp.dot(
        jnp.where(kept, 1.0, 0.0).astype(jnp.bfloat16),
        jnp.where(earlier, 1.0, 0.0).astype(jnp.bfloat16),
        preferred_element_type=jnp.float32,
    )
    slot = jnp.where(kept, before, -1.0)
    chosen = jnp.where(named, logits_ref[...], -jnp.inf)
    terms = jnp.exp(chosen - jnp.max(chosen, axis=0, keepdims=True))
    weight = jnp.where(kept, terms / jnp.sum(terms, axis=0, keepdims=True), 0.0)
    slot = jnp.concatenate([slot, slot], axis=1)
    weight = jnp.concatenate([weight, weight], axis=1)
    group = Y * CORES
    for half in range(2):
        for i in range(X):
            chunk = slice(group * (2 * i + half), group * (2 * i + half + 1))
            meta[half, group * i:group * (i + 1)] = slot[chunk]
            meta[half, PLANE + group * i:PLANE + group * (i + 1)] = weight[chunk]
    metas[0] = meta[zh]
    meta_copies = [
        remote(meta.at[1 - zh], metas.at[3], at(dz=8)),
        remote(meta.at[((z + 4) % Z) // LINE], metas.at[1], at(dz=4)),
        remote(meta.at[((z + 12) % Z) // LINE], metas.at[2], at(dz=-4)),
    ]
    for copy in meta_copies:
        copy.start()

    for copy in z_copies:
        copy.wait_recv()
    kv_steps[0].wait_recv()
    kv_steps[1].start()

    up1 = remote(block(p), block(p), at(dz=1))
    down1 = remote(block(p), block(p), at(dz=-1))
    up2 = remote(block(p - 1), block(p - 1), at(dz=1))
    down2 = remote(block(p + 1), block(p + 1), at(dz=-1))
    up3 = remote(block(0), block(0), at(dz=1))
    down3 = remote(block(3), block(3), at(dz=-1))

    def piece_a(dx, dy, lo, n):
        return wbuf.at[pl.ds(lo, n), rows(16 * ((((y + dy + Y) % Y) * 2 + c) * X + (x + dx + X) % X), 16)]

    def piece_b(dx, dy, lo, n):
        return wbuf.at[pl.ds(4 + lo, n), rows(16 * ((((x + dx + X) % X) * 2 + c) * Y + (y + dy + Y) % Y), 16)]

    def lap(region, step):
        first = [remote(region(0, 0, 4), region(0, 0, 4), step(d)) for d in (1, -1)]
        second = [
            remote(region(-1, 0, 2), region(-1, 0, 2), step(1)),
            remote(region(1, 2, 2), region(1, 2, 2), step(-1)),
        ]
        return first, second

    step_x = lambda d: at(dx=d)
    step_y = lambda d: at(dy=d)
    a1, a2 = lap(lambda d, lo, n: piece_a(d, 0, lo, n), step_x)
    b1, b2 = lap(lambda d, lo, n: piece_b(0, d, lo, n), step_y)
    second_a = {o: lap(lambda d, lo, n, o=o: piece_a(o, d, lo, n), step_y) for o in (0, 1, -1, 2)}
    second_b = {o: lap(lambda d, lo, n, o=o: piece_b(d, o, lo, n), step_x) for o in (0, 1, -1, 2)}
    c1 = {o: second_a[o][0] + second_b[o][0] for o in second_a}
    c2 = {o: second_a[o][1] + second_b[o][1] for o in second_a}

    def lane_a(d):
        return wbuf.at[pl.ds(0, 4), rows(64 * (((y + d + Y) % Y) * 2 + c), 64)]

    def lane_b(d):
        return wbuf.at[pl.ds(4, 4), rows(64 * (((x + d + X) % X) * 2 + c), 64)]

    twins = {d: [remote(lane_a(d), lane_a(d), sibling), remote(lane_b(d), lane_b(d), sibling)] for d in (0, 1, -1, 2)}
    for copy in a1 + b1 + c1[0]:
        copy.start()
    for load in loads[7:10]:
        load.wait()
    pl.when(p < 3)(up1.start)
    pl.when(p > 0)(down1.start)
    for copy in a1 + b1:
        copy.wait_recv()
    for copy in a2 + b2 + c1[1] + c1[-1]:
        copy.start()
    kv_steps[1].wait_recv()
    kv_steps[2].start()
    for copy in c1[0]:
        copy.wait_recv()
    for copy in c2[0]:
        copy.start()
    for copy in a2 + b2:
        copy.wait_recv()
    for copy in c1[2] + twins[0]:
        copy.start()
    kv_steps[2].wait_recv()
    kv_steps[3].start()

    for copy in meta_copies:
        copy.wait_recv()
    for a in range(2):
        lane = lax.broadcasted_iota(jnp.int32, (PLANE, 128), 1)
        slots = jnp.where(lane < 64, metas[2 * a, 0:PLANE], metas[2 * a + 1, 0:PLANE])
        weights = jnp.where(lane < 64, metas[2 * a, PLANE:], metas[2 * a + 1, PLANE:])
        row = lax.broadcasted_iota(jnp.int32, (PLANE, 4 * CAP, 128), 1)
        column = lax.broadcasted_iota(jnp.int32, (PLANE, 4 * CAP, 128), 2)
        same = row // CAP == 2 * a + column // 64
        hit = same & (slots[:, None, :] == (row % CAP).astype(jnp.float32))
        pick[:, 128 * a:128 * (a + 1)] = (
            jnp.where(hit, 1.0, 0.0).reshape(PLANE * 4 * CAP, 128).astype(jnp.bfloat16)
        )
        comb[:, 128 * a:128 * (a + 1)] = (
            jnp.where(hit, weights[:, None, :], 0.0).reshape(PLANE * 4 * CAP, 128).astype(jnp.bfloat16)
        )

    docs = lax.broadcasted_iota(jnp.int32, (8, 320), 0)
    key_doc = jnp.where(docs == span_ref[...], 1.0, 0.0).astype(jnp.bfloat16)
    same_doc = lax.dot_general(
        key_doc[:, 256:320], key_doc, (((0,), (0,)), ((), ())), preferred_element_type=jnp.float32
    )
    key_at = lax.broadcasted_iota(jnp.int32, (64, 320), 1)
    query_at = lax.broadcasted_iota(jnp.int32, (64, 320), 0)
    bias = jnp.where((key_at <= query_at + 256) & (same_doc > 0.5), 0.0, NEG)
    loads[10].wait()
    kv_steps[3].wait_recv()
    for g in range(4):
        head = lambda h: (g * 8 + h) * HD
        queries = jnp.concatenate([q_ref[:, head(h):head(h) + HD] for h in range(8)], axis=0)
        keys = kv[:, 0, :, g * HD:(g + 1) * HD].reshape(5 * 64, HD)
        values = kv[:, 1, :, g * HD:(g + 1) * HD].reshape(5 * 64, HD)
        scores = lax.dot_general(
            queries, keys, (((1,), (1,)), ((), ())), preferred_element_type=jnp.float32
        ) * (1.0 / HD**0.5)
        scores = (scores.reshape(8, 64, 320) + bias[None]).reshape(512, 320)
        terms = jnp.exp(scores - jnp.max(scores, axis=-1, keepdims=True))
        probs = (terms / jnp.sum(terms, axis=-1, keepdims=True)).astype(jnp.bfloat16)
        out = jnp.dot(probs, values, preferred_element_type=jnp.float32).astype(jnp.bfloat16)
        for h in range(8):
            att[:, head(h):head(h) + HD] = out[64 * h:64 * (h + 1)]

    for copy in c1[1] + c1[-1]:
        copy.wait_recv()
    for copy in c2[1] + c2[-1]:
        copy.start()
    for copy in c1[2]:
        copy.wait_recv()
    for copy in c2[2] + twins[1] + twins[-1]:
        copy.start()
    pl.when(p > 0)(up1.wait_recv)
    pl.when(p < 3)(down1.wait_recv)
    pl.when((p > 0) & (p < 3))(up2.start)
    pl.when((p > 0) & (p < 3))(down2.start)
    for o in c2:
        for copy in c2[o]:
            copy.wait_recv()
    for copy in twins[2]:
        copy.start()
    for d in (0, 1, -1, 2):
        for copy in twins[d]:
            copy.wait_recv()

    for load in loads[11:]:
        load.wait()
    for n in range(4):
        cols = slice(512 * n, 512 * (n + 1))
        acc = res_ref[:, cols].astype(jnp.float32)
        for t in range(8):
            acc = acc + jnp.dot(
                att[:, 512 * t:512 * (t + 1)], wbuf[t, :, cols], preferred_element_type=jnp.float32
            )
        total[:, cols] = acc
    hidden = total[...]
    square = jnp.mean(hidden * hidden, axis=-1, keepdims=True)
    normed = (hidden * lax.rsqrt(square + EPSILON) * gain_ref[...]).astype(jnp.bfloat16)
    for q in range(CHUNKS):
        tok[q, 0:64] = normed[:, width * q:width * (q + 1)]

    near = [
        (
            copy_to(tok.at[q, pl.ds(0, 64)], tok.at[q, pl.ds(64, 64)], z_send.at[q, 0], z_recv.at[q, 0], at(dz=4)),
            copy_to(tok.at[q, pl.ds(0, 64)], tok.at[q, pl.ds(128, 64)], z_send.at[q, 1], z_recv.at[q, 1], at(dz=-4)),
        )
        for q in range(CHUNKS)
    ]
    across = [
        (
            copy_to(tok.at[q, pl.ds(64, 32)], tok.at[q, pl.ds(192, 32)], h_send.at[q, 0], h_recv.at[q, 0], at(dz=4)),
            copy_to(tok.at[q, pl.ds(160, 32)], tok.at[q, pl.ds(224, 32)], h_send.at[q, 1], h_recv.at[q, 1], at(dz=-4)),
        )
        for q in range(CHUNKS)
    ]
    for q in range(CHUNKS):
        for copy in near[q]:
            copy.start()
    hidden_ref[...] = hidden.astype(jnp.bfloat16)

    def spread(src, dst, q, ss, rs):
        def go(o, _):
            peer, where = partner(o)
            copy_to(
                src.at[q, rows(32 * peer, 32)], dst.at[q, rows(32 * me, 32)], ss.at[q], rs.at[q], where
            ).start()
            return 0

        lax.fori_loop(1, PLANE, go, 0)
        dst[q, rows(32 * me, 32)] = src[q, rows(32 * me, 32)]

    def whole(src, dst, q, ss, rs):
        every = pl.ds(0, 32 * (PLANE - 1))
        return copy_to(src.at[q, every], dst.at[q, every], ss.at[q], rs.at[q], at(dz=1))

    def dispatch(q):
        for copy in across[q]:
            copy.wait_recv()

        def tile(i, _):
            part_rows = pl.ds(pl.multiple_of(i * 256, 256), 256)
            sent[q, part_rows] = jnp.dot(
                pick[part_rows], tok[q], preferred_element_type=jnp.float32
            ).astype(jnp.bfloat16)
            return 0

        lax.fori_loop(0, 4, tile, 0)
        spread(sent, got, q, p_send, p_recv)

    for q in range(CHUNKS):
        for copy in near[q]:
            copy.wait_recv()
        for copy in across[q]:
            copy.start()
        if q >= 1:
            dispatch(q - 1)
    dispatch(CHUNKS - 1)
    pl.when(p > 1)(up2.wait_recv)
    pl.when(p < 2)(down2.wait_recv)
    pl.when(p == 2)(up3.start)
    pl.when(p == 1)(down3.start)

    pl.when(p == 3)(up3.wait_recv)
    pl.when(p == 0)(down3.wait_recv)
    transposed = (((1,), (1,)), ((), ()))
    for q in range(CHUNKS):
        whole(sent, got, q, p_send, p_recv).wait_recv()
        cols = slice(width * q, width * (q + 1))

        def tile(i, _, q=q, cols=cols):
            part_rows = pl.ds(pl.multiple_of(i * 256, 256), 256)
            for m in range(2):
                value = lax.dot_general(
                    got[q, part_rows], wv[m, :, cols], transposed, preferred_element_type=jnp.float32
                )
                if q == 0:
                    accum[m, part_rows] = value
                else:
                    accum[m, part_rows] += value
            return 0

        lax.fori_loop(0, 4, tile, 0)

    def activate(i, _):
        part_rows = pl.ds(pl.multiple_of(i * 256, 256), 256)
        gate = accum[0, part_rows]
        act[part_rows] = (gate / (1.0 + jnp.exp(-gate)) * accum[1, part_rows]).astype(jnp.bfloat16)
        return 0

    lax.fori_loop(0, 4, activate, 0)

    for q in range(CHUNKS):
        cols = slice(width * q, width * (q + 1))

        def tile(i, _, q=q, cols=cols):
            part_rows = pl.ds(pl.multiple_of(i * 256, 256), 256)
            made[q, part_rows] = jnp.dot(
                act[part_rows], wv[2, :, cols], preferred_element_type=jnp.float32
            ).astype(jnp.bfloat16)
            return 0

        lax.fori_loop(0, 4, tile, 0)
        spread(made, back, q, r_send, r_recv)

    def half_copies(q):
        return (
            copy_to(far.at[q, 0, pl.ds(0, 32)], home.at[q, 0, pl.ds(0, 32)], f_send.at[q, 0], f_recv.at[q, 0], at(dz=4)),
            copy_to(far.at[q, 0, pl.ds(32, 32)], home.at[q, 0, pl.ds(32, 32)], f_send.at[q, 1], f_recv.at[q, 1], at(dz=-4)),
        )

    def home_copies(q):
        return (
            copy_to(far.at[q, 1], home.at[q, 1], o_send.at[q, 0], o_recv.at[q, 0], at(dz=-4)),
            copy_to(far.at[q, 2], home.at[q, 2], o_send.at[q, 1], o_recv.at[q, 1], at(dz=4)),
        )

    def combine(q):
        whole(made, back, q, r_send, r_recv).wait_recv()
        part[q] = lax.dot_general(
            comb[...], back[q], (((0,), (0,)), ((), ())), preferred_element_type=jnp.float32
        )
        far[q, 0] = part[q, 192:256].astype(jnp.bfloat16)
        for copy in half_copies(q):
            copy.start()

    def relay(q):
        for copy in half_copies(q):
            copy.wait_recv()
        ahead, behind = part[q, 128:192], part[q, 64:128]
        far[q, 2, 0:32] = (ahead[0:32] + home[q, 0, 0:32].astype(jnp.float32)).astype(jnp.bfloat16)
        far[q, 2, 32:64] = ahead[32:64].astype(jnp.bfloat16)
        far[q, 1, 0:32] = behind[0:32].astype(jnp.bfloat16)
        far[q, 1, 32:64] = (behind[32:64] + home[q, 0, 32:64].astype(jnp.float32)).astype(jnp.bfloat16)
        for copy in home_copies(q):
            copy.start()

    def finish(q):
        for copy in home_copies(q):
            copy.wait_recv()
        total = part[q, 0:64] + home[q, 1].astype(jnp.float32) + home[q, 2].astype(jnp.float32)
        out_ref[:, width * q:width * (q + 1)] = total.astype(jnp.bfloat16)

    for step in range(CHUNKS + 2):
        if step < CHUNKS:
            combine(step)
        if 0 <= step - 1 < CHUNKS:
            relay(step - 1)
        if 0 <= step - 2 < CHUNKS:
            finish(step - 2)

    for q in range(CHUNKS):
        for copy in near[q] + across[q] + half_copies(q) + home_copies(q):
            copy.wait_send()
        whole(sent, got, q, p_send, p_recv).wait_send()
        whole(made, back, q, r_send, r_recv).wait_send()
    for copy in kv_steps + z_copies + meta_copies + a1 + b1 + a2 + b2:
        copy.wait_send()
    for o in c1:
        for copy in c1[o] + c2[o]:
            copy.wait_send()
    for d in (0, 1, -1, 2):
        for copy in twins[d]:
            copy.wait_send()
    pl.when(p < 3)(up1.wait_send)
    pl.when(p > 0)(down1.wait_send)
    pl.when((p > 0) & (p < 3))(up2.wait_send)
    pl.when((p > 0) & (p < 3))(down2.wait_send)
    pl.when(p == 2)(up3.wait_send)
    pl.when(p == 1)(down3.wait_send)


def layer(*args):
    d = args[4].shape[1]
    width = d // CHUNKS
    slots = PLANE * 4 * CAP
    units = SUB * 96
    dma = lambda *shape: pltpu.SemaphoreType.DMA(shape)
    half = lambda *shape: pltpu.VMEM(shape, jnp.bfloat16)
    full = lambda *shape: pltpu.VMEM(shape, jnp.float32)
    return pl.pallas_call(
        layer_kernel,
        out_shape=(jax.ShapeDtypeStruct((64, d), jnp.bfloat16), jax.ShapeDtypeStruct((64, d), jnp.bfloat16)),
        in_specs=[ANY] * len(args),
        out_specs=(VMEM, VMEM),
        scratch_shapes=[
            half(64, 4096), half(5, 2, 64, 512), pltpu.VMEM((1, 320), jnp.int32), half(64, d), full(1, d),
            full(64, 64), pltpu.VMEM((8, 64), jnp.int32), pltpu.VMEM((8, 64), jnp.int32),
            full(2, 64, 128), full(4, 64, 128),
            half(LINE, 512, d), half(64, 4096), full(64, d), half(3, units, d),
            half(slots, 256), half(slots, 256), half(CHUNKS, 256, width),
            half(CHUNKS, slots, width), half(CHUNKS, slots, width),
            full(2, slots, units), half(slots, units),
            half(CHUNKS, slots, width), half(CHUNKS, slots, width),
            full(CHUNKS, 256, width), half(CHUNKS, 3, 64, width), half(CHUNKS, 3, 64, width),
            dma(80), dma(80), dma(13),
            dma(CHUNKS, 2), dma(CHUNKS, 2), dma(CHUNKS, 2), dma(CHUNKS, 2),
            dma(CHUNKS), dma(CHUNKS), dma(CHUNKS), dma(CHUNKS),
            dma(CHUNKS, 2), dma(CHUNKS, 2), dma(CHUNKS, 2), dma(CHUNKS, 2),
        ],
        compiler_params=pltpu.CompilerParams(
            collective_id=0, has_side_effects=True, vmem_limit_bytes=60 * 2**20
        ),
        cost_estimate=pl.CostEstimate(flops=7 * 10**9, bytes_accessed=3 * 10**7, transcendentals=10**6),
    )(*args)


def shards(
    queries, key_heads, value_heads, doc_ids, residual, w_out, norm_gain, router_logits, expert_ids, keep_mask,
    w_gate, w_up, w_down,
):
    s = lax.axis_index("seq")
    doc = jnp.pad(doc_ids[0], (256, 0), constant_values=-1)
    span = lax.dynamic_slice(doc, (64 * s,), (320,))[None]
    hidden, out = layer(
        queries[0], key_heads[0], value_heads[0], span, residual[0], norm_gain[None], router_logits[0].T,
        expert_ids[0].T, keep_mask[0].T, w_out, w_gate[0], w_up[0], w_down[0],
    )
    return hidden[None], out[None]


def solution(mesh):
    split = P("exp", "seq", None)
    return jax.shard_map(
        shards,
        mesh=mesh,
        in_specs=(split, split, split, P("exp", None), split, P("seq", None), P()) + (split,) * 6,
        out_specs=(split, split),
        check_vma=False,
    )
```

```python
import jax
import jax.numpy as jnp
from jax import lax
from jax.experimental import pallas as pl
from jax.experimental.pallas import tpu as pltpu
from jax.sharding import PartitionSpec as P

MESH = pl.DeviceIdType.MESH
HD = 128
CAP = 8
X, Y, Z, LINE, CORES = 4, 4, 16, 8, 2
PLANE = X * Y * CORES
SUB = 4
CHUNKS = 4
BATCH = 2 * CAP
STEPS = 2 * CHUNKS
EPSILON = 1e-06
NEG = -1e30
ANY = pl.BlockSpec(memory_space=pl.ANY)
VMEM = pl.BlockSpec(memory_space=pltpu.VMEM)
Z_OFFSETS = (1, -1, 2, -2, 3, -3, 4)


def place():
    s = lax.axis_index("seq")
    e = lax.axis_index("exp")
    c = e % 2
    y = (e // 2) % Y
    zh = (e // (2 * Y)) % 2
    x = e // (4 * Y)
    return x, y, zh * LINE + s, c


def device(x, y, z, c):
    x, y, z = x % X, y % Y, z % Z
    return {"seq": z % LINE, "exp": ((x * 2 + z // LINE) * Y + y) * 2 + c}


def rows(start, count):
    return pl.ds(pl.multiple_of(start, 16), count)


def layer_kernel(
    q_hbm, k_hbm, v_hbm, span_hbm, res_hbm, gain_hbm, logits_hbm, ids_hbm, keep_hbm, wout_ref, wg_ref, wu_ref, wd_ref,
    hidden_ref, out_ref,
    q_ref, kv, span_ref, res_ref, gain_ref, logits_ref, ids_ref, keep_ref, meta, metas,
    wbuf, att, total, wv, pick, comb, tok, sent, got, accum, act, made, back, own, far, home,
    send, recv, local,
    z_send, z_recv, h_send, h_recv, p_send, p_recv, r_send, r_recv, f_send, f_recv, o_send, o_recv,
):
    x, y, z, c = place()
    s = z % LINE
    zh = z // LINE
    p = z % SUB
    me = (x * Y + y) * CORES + c
    width = tok.shape[2]

    def at(dx=0, dy=0, dz=0):
        return device(x + dx + X, y + dy + Y, z + dz + Z, c)

    def partner(o):
        dx = o % X
        px = (x + dx) % X
        py = (y + o // (X * CORES) + dx) % Y
        pc = (c + o // X) % CORES
        return (px * Y + py) * CORES + pc, device(px, py, z, pc)

    sibling = device(x, y, z, 1 - c)
    counter = [0]

    def remote(src, dst, peer):
        i = counter[0]
        counter[0] += 1
        return copy_to(src, dst, send.at[i], recv.at[i], peer)

    def copy_to(src, dst, ss, rs, peer):
        return pltpu.make_async_remote_copy(
            src_ref=src, dst_ref=dst, send_sem=ss, recv_sem=rs, device_id=peer, device_id_type=MESH
        )

    def block(m, owner):
        return wv.at[m, rows(96 * ((owner + SUB) % SUB), 96)]

    ja = (y * 2 + c) * X + x
    jb = (x * 2 + c) * Y + y
    mine = jnp.where(s < 4, ja, jb) * 16
    piece = wbuf.at[s, rows(mine, 16)]
    moves = [
        (k_hbm, kv.at[4, 0]), (v_hbm, kv.at[4, 1]), (wout_ref.at[rows(mine, 16)], piece),
        (ids_hbm, ids_ref), (keep_hbm, keep_ref), (logits_hbm, logits_ref), (span_hbm, span_ref),
        (wg_ref, wv.at[0, rows(96 * p, 96)]), (wu_ref, wv.at[1, rows(96 * p, 96)]),
        (wd_ref, wv.at[2, rows(96 * p, 96)]),
        (q_hbm, q_ref), (res_hbm, res_ref), (gain_hbm, gain_ref),
    ]
    loads = [pltpu.make_async_copy(src, dst, local.at[i]) for i, (src, dst) in enumerate(moves)]
    for load in loads:
        load.start()

    barrier = pltpu.get_barrier_semaphore()
    for d in (1, -1, 2, -2, 3, -3, 4, -4, 8):
        pl.semaphore_signal(barrier, inc=1, device_id=at(dz=d), device_id_type=MESH)

    def greet(o, _):
        pl.semaphore_signal(barrier, inc=1, device_id=partner(o)[1], device_id_type=MESH)
        return 0

    lax.fori_loop(1, PLANE, greet, 0)
    pl.semaphore_wait(barrier, 9 + PLANE - 1)

    kv_steps = [remote(kv.at[4 - d], kv.at[3 - d], at(dz=1)) for d in range(4)]
    z_copies = [remote(piece, piece, at(dz=d)) for d in Z_OFFSETS]
    for load in loads[:3]:
        load.wait()
    for copy in z_copies:
        copy.start()
    kv_steps[0].start()

    for load in loads[3:7]:
        load.wait()
    experts = logits_ref.shape[1]
    expert = lax.broadcasted_iota(jnp.int32, (experts, 64), 0)
    named = expert == ids_ref[0:1, :]
    kept = named & (keep_ref[0:1, :] == 1)
    for k in range(1, ids_ref.shape[0]):
        hit = expert == ids_ref[k:k + 1, :]
        named = named | hit
        kept = kept | (hit & (keep_ref[k:k + 1, :] == 1))
    earlier = lax.broadcasted_iota(jnp.int32, (64, 64), 0) < lax.broadcasted_iota(jnp.int32, (64, 64), 1)
    before = jnp.dot(
        jnp.where(kept, 1.0, 0.0).astype(jnp.bfloat16),
        jnp.where(earlier, 1.0, 0.0).astype(jnp.bfloat16),
        preferred_element_type=jnp.float32,
    )
    slot = jnp.where(kept, before, -1.0)
    chosen = jnp.where(named, logits_ref[...], -jnp.inf)
    terms = jnp.exp(chosen - jnp.max(chosen, axis=0, keepdims=True))
    weight = jnp.where(kept, terms / jnp.sum(terms, axis=0, keepdims=True), 0.0)
    slot = jnp.concatenate([slot, slot], axis=1)
    weight = jnp.concatenate([weight, weight], axis=1)
    group = Y * CORES
    for half in range(2):
        for i in range(X):
            chunk = slice(group * (2 * i + half), group * (2 * i + half + 1))
            meta[half, group * i:group * (i + 1)] = slot[chunk]
            meta[half, PLANE + group * i:PLANE + group * (i + 1)] = weight[chunk]
    metas[0] = meta[zh]
    meta_copies = [
        remote(meta.at[1 - zh], metas.at[1], at(dz=8)),
        remote(meta.at[((z + 4) % Z) // LINE], metas.at[2], at(dz=4)),
        remote(meta.at[((z + 12) % Z) // LINE], metas.at[3], at(dz=-4)),
    ]
    for copy in meta_copies:
        copy.start()

    kv_steps[0].wait_recv()
    kv_steps[1].start()
    for copy in z_copies:
        copy.wait_recv()

    up1 = [remote(block(m, p), block(m, p), at(dz=1)) for m in range(3)]
    down1 = [remote(block(m, p), block(m, p), at(dz=-1)) for m in range(3)]
    up2 = [remote(block(m, p - 1), block(m, p - 1), at(dz=1)) for m in range(3)]
    down2 = [remote(block(m, p + 1), block(m, p + 1), at(dz=-1)) for m in range(3)]
    up3 = [remote(block(m, 0), block(m, 0), at(dz=1)) for m in range(3)]
    down3 = [remote(block(m, 3), block(m, 3), at(dz=-1)) for m in range(3)]

    def pass_on(m):
        pl.when(p > 0)(up1[m].wait_recv)
        pl.when(p < 3)(down1[m].wait_recv)
        pl.when((p > 0) & (p < 3))(up2[m].start)
        pl.when((p > 0) & (p < 3))(down2[m].start)

    def pass_last(m):
        pl.when(p > 1)(up2[m].wait_recv)
        pl.when(p < 2)(down2[m].wait_recv)
        pl.when(p == 2)(up3[m].start)
        pl.when(p == 1)(down3[m].start)

    def piece_a(dx, dy, lo, n):
        return wbuf.at[pl.ds(lo, n), rows(16 * ((((y + dy + Y) % Y) * 2 + c) * X + (x + dx + X) % X), 16)]

    def piece_b(dx, dy, lo, n):
        return wbuf.at[pl.ds(4 + lo, n), rows(16 * ((((x + dx + X) % X) * 2 + c) * Y + (y + dy + Y) % Y), 16)]

    def lap(region, step):
        first = [remote(region(0, 0, 4), region(0, 0, 4), step(d)) for d in (1, -1)]
        second = [
            remote(region(-1, 0, 2), region(-1, 0, 2), step(1)),
            remote(region(1, 2, 2), region(1, 2, 2), step(-1)),
        ]
        return first, second

    step_x = lambda d: at(dx=d)
    step_y = lambda d: at(dy=d)
    a1, a2 = lap(lambda d, lo, n: piece_a(d, 0, lo, n), step_x)
    b1, b2 = lap(lambda d, lo, n: piece_b(0, d, lo, n), step_y)
    second_a = {o: lap(lambda d, lo, n, o=o: piece_a(o, d, lo, n), step_y) for o in (0, 1, -1, 2)}
    second_b = {o: lap(lambda d, lo, n, o=o: piece_b(d, o, lo, n), step_x) for o in (0, 1, -1, 2)}
    c1 = {o: second_a[o][0] + second_b[o][0] for o in second_a}
    c2 = {o: second_a[o][1] + second_b[o][1] for o in second_a}

    def lane_a(d):
        return wbuf.at[pl.ds(0, 4), rows(64 * (((y + d + Y) % Y) * 2 + c), 64)]

    def lane_b(d):
        return wbuf.at[pl.ds(4, 4), rows(64 * (((x + d + X) % X) * 2 + c), 64)]

    twins = {d: [remote(lane_a(d), lane_a(d), sibling), remote(lane_b(d), lane_b(d), sibling)] for d in (0, 1, -1, 2)}
    for copy in a1 + b1 + c1[0]:
        copy.start()
    for load in loads[7:10]:
        load.wait()
    for m in range(3):
        pl.when(p < 3)(up1[m].start)
        pl.when(p > 0)(down1[m].start)
    for copy in a1 + b1:
        copy.wait_recv()
    for copy in a2 + b2 + c1[1] + c1[-1]:
        copy.start()
    kv_steps[1].wait_recv()
    kv_steps[2].start()
    for copy in c1[0]:
        copy.wait_recv()
    for copy in c2[0]:
        copy.start()
    for copy in a2 + b2:
        copy.wait_recv()
    for copy in c1[2] + twins[0]:
        copy.start()
    kv_steps[2].wait_recv()
    kv_steps[3].start()

    for copy in meta_copies:
        copy.wait_recv()
    for a in range(2):
        lane = lax.broadcasted_iota(jnp.int32, (PLANE, 128), 1)
        slots = jnp.where(lane < 64, metas[2 * a, 0:PLANE], metas[2 * a + 1, 0:PLANE])
        weights = jnp.where(lane < 64, metas[2 * a, PLANE:], metas[2 * a + 1, PLANE:])
        row = lax.broadcasted_iota(jnp.int32, (PLANE, BATCH, 128), 1)
        column = lax.broadcasted_iota(jnp.int32, (PLANE, BATCH, 128), 2)
        hit = (row // CAP == column // 64) & (slots[:, None, :] == (row % CAP).astype(jnp.float32))
        pick[a] = jnp.where(hit, 1.0, 0.0).reshape(PLANE * BATCH, 128).astype(jnp.bfloat16)
        comb[a] = jnp.where(hit, weights[:, None, :], 0.0).reshape(PLANE * BATCH, 128).astype(jnp.bfloat16)

    docs = lax.broadcasted_iota(jnp.int32, (8, 320), 0)
    key_doc = jnp.where(docs == span_ref[...], 1.0, 0.0).astype(jnp.bfloat16)
    same_doc = lax.dot_general(
        key_doc[:, 256:320], key_doc, (((0,), (0,)), ((), ())), preferred_element_type=jnp.float32
    )
    key_at = lax.broadcasted_iota(jnp.int32, (64, 320), 1)
    query_at = lax.broadcasted_iota(jnp.int32, (64, 320), 0)
    bias = jnp.where((key_at <= query_at + 256) & (same_doc > 0.5), 0.0, NEG)
    loads[10].wait()

    def attend(g):
        head = lambda h: (g * 8 + h) * HD
        queries = jnp.concatenate([q_ref[:, head(h):head(h) + HD] for h in range(8)], axis=0)
        keys = kv[:, 0, :, g * HD:(g + 1) * HD].reshape(5 * 64, HD)
        values = kv[:, 1, :, g * HD:(g + 1) * HD].reshape(5 * 64, HD)
        scores = lax.dot_general(
            queries, keys, (((1,), (1,)), ((), ())), preferred_element_type=jnp.float32
        ) * (1.0 / HD**0.5)
        scores = (scores.reshape(8, 64, 320) + bias[None]).reshape(512, 320)
        terms = jnp.exp(scores - jnp.max(scores, axis=-1, keepdims=True))
        probs = (terms / jnp.sum(terms, axis=-1, keepdims=True)).astype(jnp.bfloat16)
        out = jnp.dot(probs, values, preferred_element_type=jnp.float32).astype(jnp.bfloat16)
        for h in range(8):
            att[:, head(h):head(h) + HD] = out[64 * h:64 * (h + 1)]

    for copy in c1[1] + c1[-1]:
        copy.wait_recv()
    for copy in c2[1] + c2[-1]:
        copy.start()
    pass_on(0)
    for copy in c1[2]:
        copy.wait_recv()
    for copy in c2[2] + twins[1] + twins[-1]:
        copy.start()
    pass_on(1)
    kv_steps[3].wait_recv()
    for g in range(4):
        attend(g)
    for o in c2:
        for copy in c2[o]:
            copy.wait_recv()
    for copy in twins[2]:
        copy.start()
    pass_on(2)
    for d in (0, 1, -1, 2):
        for copy in twins[d]:
            copy.wait_recv()

    for load in loads[11:]:
        load.wait()
    for n in range(4):
        cols = slice(512 * n, 512 * (n + 1))
        acc = res_ref[:, cols].astype(jnp.float32)
        for t in range(8):
            acc = acc + jnp.dot(
                att[:, 512 * t:512 * (t + 1)], wbuf[t, :, cols], preferred_element_type=jnp.float32
            )
        total[:, cols] = acc
    hidden = total[...]
    square = jnp.mean(hidden * hidden, axis=-1, keepdims=True)
    normed = (hidden * lax.rsqrt(square + EPSILON) * gain_ref[...]).astype(jnp.bfloat16)
    for q in range(CHUNKS):
        tok[q, 0:64] = normed[:, width * q:width * (q + 1)]

    near = [
        (
            copy_to(tok.at[q, pl.ds(0, 64)], tok.at[q, pl.ds(128, 64)], z_send.at[q, 0], z_recv.at[q, 0], at(dz=4)),
            copy_to(tok.at[q, pl.ds(0, 64)], tok.at[q, pl.ds(192, 64)], z_send.at[q, 1], z_recv.at[q, 1], at(dz=-4)),
        )
        for q in range(CHUNKS)
    ]
    across = [
        (
            copy_to(tok.at[q, pl.ds(128, 32)], tok.at[q, pl.ds(64, 32)], h_send.at[q, 0], h_recv.at[q, 0], at(dz=4)),
            copy_to(tok.at[q, pl.ds(224, 32)], tok.at[q, pl.ds(96, 32)], h_send.at[q, 1], h_recv.at[q, 1], at(dz=-4)),
        )
        for q in range(CHUNKS)
    ]
    for copy in near[0]:
        copy.start()
    hidden_ref[...] = hidden.astype(jnp.bfloat16)

    def spread(src, dst, i, ss, rs):
        def go(o, _):
            peer, where = partner(o)
            copy_to(
                src.at[i, rows(BATCH * peer, BATCH)], dst.at[i, rows(BATCH * me, BATCH)], ss.at[i], rs.at[i], where
            ).start()
            return 0

        lax.fori_loop(1, PLANE, go, 0)
        dst[i, rows(BATCH * me, BATCH)] = src[i, rows(BATCH * me, BATCH)]

    def whole(src, dst, i, ss, rs):
        every = pl.ds(0, BATCH * (PLANE - 1))
        return copy_to(src.at[i, every], dst.at[i, every], ss.at[i], rs.at[i], at(dz=1))

    def tile_rows(i):
        return pl.ds(pl.multiple_of(i * 256, 256), 256)

    def dispatch(b, q):
        def tile(i, _):
            sent[b * CHUNKS + q, tile_rows(i)] = jnp.dot(
                pick[b, tile_rows(i)], tok[q, 128 * b:128 * (b + 1)], preferred_element_type=jnp.float32
            ).astype(jnp.bfloat16)
            return 0

        lax.fori_loop(0, 2, tile, 0)
        spread(sent, got, b * CHUNKS + q, p_send, p_recv)

    for q in range(CHUNKS):
        if q < CHUNKS - 1:
            for copy in near[q]:
                copy.wait_send()
            for copy in near[q + 1]:
                copy.start()
        for copy in near[q]:
            copy.wait_recv()
        for copy in across[q]:
            copy.start()
        dispatch(1, q)
        if q >= 1:
            for copy in across[q - 1]:
                copy.wait_recv()
            dispatch(0, q - 1)
    for copy in across[CHUNKS - 1]:
        copy.wait_recv()
    dispatch(0, CHUNKS - 1)
    for m in range(3):
        pass_last(m)

    def last_here(m):
        pl.when(p == 3)(up3[m].wait_recv)
        pl.when(p == 0)(down3[m].wait_recv)

    last_here(0)
    last_here(1)
    transposed = (((1,), (1,)), ((), ()))

    def gate_up(b, q):
        step = b * CHUNKS + q
        whole(sent, got, step, p_send, p_recv).wait_recv()
        cols = slice(width * q, width * (q + 1))

        def tile(i, _):
            for m in range(2):
                value = lax.dot_general(
                    got[step, tile_rows(i)], wv[m, :, cols], transposed, preferred_element_type=jnp.float32
                )
                if q == 0:
                    accum[b, m, tile_rows(i)] = value
                else:
                    accum[b, m, tile_rows(i)] += value
            return 0

        lax.fori_loop(0, 2, tile, 0)

    def activate(b):
        def tile(i, _):
            gate = accum[b, 0, tile_rows(i)]
            act[b, tile_rows(i)] = (gate / (1.0 + jnp.exp(-gate)) * accum[b, 1, tile_rows(i)]).astype(jnp.bfloat16)
            return 0

        lax.fori_loop(0, 2, tile, 0)

    def down(b, q):
        cols = slice(width * q, width * (q + 1))

        def tile(i, _):
            made[b * CHUNKS + q, tile_rows(i)] = jnp.dot(
                act[b, tile_rows(i)], wv[2, :, cols], preferred_element_type=jnp.float32
            ).astype(jnp.bfloat16)
            return 0

        lax.fori_loop(0, 2, tile, 0)

    def give_back(step):
        if step > 0:
            whole(made, back, step - 1, r_send, r_recv).wait_send()
        spread(made, back, step, r_send, r_recv)

    def half_copies(q):
        return (
            copy_to(far.at[q, 0, pl.ds(0, 32)], home.at[q, 0, pl.ds(0, 32)], f_send.at[q, 0], f_recv.at[q, 0], at(dz=4)),
            copy_to(far.at[q, 0, pl.ds(32, 32)], home.at[q, 0, pl.ds(32, 32)], f_send.at[q, 1], f_recv.at[q, 1], at(dz=-4)),
        )

    def home_copies(q):
        return (
            copy_to(far.at[q, 1], home.at[q, 1], o_send.at[q, 0], o_recv.at[q, 0], at(dz=-4)),
            copy_to(far.at[q, 2], home.at[q, 2], o_send.at[q, 1], o_recv.at[q, 1], at(dz=4)),
        )

    def combine(b, q):
        step = b * CHUNKS + q
        whole(made, back, step, r_send, r_recv).wait_recv()
        part = lax.dot_general(
            comb[b], back[step], (((0,), (0,)), ((), ())), preferred_element_type=jnp.float32
        )
        if b == 0:
            own[q] = part[0:64]
            far[q, 0] = part[64:128].astype(jnp.bfloat16)
            for copy in half_copies(q):
                copy.start()
        else:
            for copy in half_copies(q):
                copy.wait_recv()
            far[q, 1, 0:32] = part[0:32].astype(jnp.bfloat16)
            far[q, 1, 32:64] = (part[32:64] + home[q, 0, 32:64].astype(jnp.float32)).astype(jnp.bfloat16)
            far[q, 2, 0:32] = (part[64:96] + home[q, 0, 0:32].astype(jnp.float32)).astype(jnp.bfloat16)
            far[q, 2, 32:64] = part[96:128].astype(jnp.bfloat16)
            for copy in home_copies(q):
                copy.start()

    def finish(q):
        for copy in home_copies(q):
            copy.wait_recv()
        total = own[q] + home[q, 1].astype(jnp.float32) + home[q, 2].astype(jnp.float32)
        out_ref[:, width * q:width * (q + 1)] = total.astype(jnp.bfloat16)

    for q in range(CHUNKS):
        gate_up(1, q)
        gate_up(0, q)
    activate(0)
    last_here(2)
    down(0, 0)
    give_back(0)
    for q in range(1, CHUNKS):
        down(0, q)
    give_back(1)
    activate(1)
    give_back(2)
    combine(0, 0)
    down(1, 0)
    down(1, 1)
    give_back(3)
    combine(0, 1)
    down(1, 2)
    down(1, 3)
    give_back(4)
    combine(0, 2)
    give_back(5)
    combine(0, 3)
    give_back(6)
    combine(1, 0)
    give_back(7)
    combine(1, 1)
    finish(0)
    combine(1, 2)
    finish(1)
    combine(1, 3)
    finish(2)
    finish(3)

    for copy in near[CHUNKS - 1]:
        copy.wait_send()
    for q in range(CHUNKS):
        for copy in across[q] + half_copies(q) + home_copies(q):
            copy.wait_send()
    for step in range(STEPS):
        whole(sent, got, step, p_send, p_recv).wait_send()
    whole(made, back, STEPS - 1, r_send, r_recv).wait_send()
    for copy in kv_steps + z_copies + meta_copies + a1 + b1 + a2 + b2:
        copy.wait_send()
    for o in c1:
        for copy in c1[o] + c2[o] + twins[o]:
            copy.wait_send()
    for m in range(3):
        pl.when(p < 3)(up1[m].wait_send)
        pl.when(p > 0)(down1[m].wait_send)
        pl.when((p > 0) & (p < 3))(up2[m].wait_send)
        pl.when((p > 0) & (p < 3))(down2[m].wait_send)
        pl.when(p == 2)(up3[m].wait_send)
        pl.when(p == 1)(down3[m].wait_send)


def layer(*args):
    d = args[4].shape[1]
    width = d // CHUNKS
    slots = PLANE * BATCH
    units = SUB * 96
    dma = lambda *shape: pltpu.SemaphoreType.DMA(shape)
    half = lambda *shape: pltpu.VMEM(shape, jnp.bfloat16)
    full = lambda *shape: pltpu.VMEM(shape, jnp.float32)
    return pl.pallas_call(
        layer_kernel,
        out_shape=(jax.ShapeDtypeStruct((64, d), jnp.bfloat16), jax.ShapeDtypeStruct((64, d), jnp.bfloat16)),
        in_specs=[ANY] * len(args),
        out_specs=(VMEM, VMEM),
        scratch_shapes=[
            half(64, 4096), half(5, 2, 64, 512), pltpu.VMEM((1, 320), jnp.int32), half(64, d), full(1, d),
            full(64, 64), pltpu.VMEM((8, 64), jnp.int32), pltpu.VMEM((8, 64), jnp.int32),
            full(2, 64, 128), full(4, 64, 128),
            half(LINE, 512, d), half(64, 4096), full(64, d), half(3, units, d),
            half(2, slots, 128), half(2, slots, 128), half(CHUNKS, 256, width),
            half(STEPS, slots, width), half(STEPS, slots, width),
            full(2, 2, slots, units), half(2, slots, units),
            half(STEPS, slots, width), half(STEPS, slots, width),
            full(CHUNKS, 64, width), half(CHUNKS, 3, 64, width), half(CHUNKS, 3, 64, width),
            dma(96), dma(96), dma(13),
            dma(CHUNKS, 2), dma(CHUNKS, 2), dma(CHUNKS, 2), dma(CHUNKS, 2),
            dma(STEPS), dma(STEPS), dma(STEPS), dma(STEPS),
            dma(CHUNKS, 2), dma(CHUNKS, 2), dma(CHUNKS, 2), dma(CHUNKS, 2),
        ],
        compiler_params=pltpu.CompilerParams(
            collective_id=0, has_side_effects=True, vmem_limit_bytes=60 * 2**20
        ),
        cost_estimate=pl.CostEstimate(flops=7 * 10**9, bytes_accessed=3 * 10**7, transcendentals=10**6),
    )(*args)


def shards(
    queries, key_heads, value_heads, doc_ids, residual, w_out, norm_gain, router_logits, expert_ids, keep_mask,
    w_gate, w_up, w_down,
):
    s = lax.axis_index("seq")
    doc = jnp.pad(doc_ids[0], (256, 0), constant_values=-1)
    span = lax.dynamic_slice(doc, (64 * s,), (320,))[None]
    hidden, out = layer(
        queries[0], key_heads[0], value_heads[0], span, residual[0], norm_gain[None], router_logits[0].T,
        expert_ids[0].T, keep_mask[0].T, w_out, w_gate[0], w_up[0], w_down[0],
    )
    return hidden[None], out[None]


def solution(mesh):
    split = P("exp", "seq", None)
    return jax.shard_map(
        shards,
        mesh=mesh,
        in_specs=(split, split, split, P("exp", None), split, P("seq", None), P()) + (split,) * 6,
        out_specs=(split, split),
        check_vma=False,
    )
```

```python
import jax
import jax.numpy as jnp
from jax import lax
from jax.experimental import pallas as pl
from jax.experimental.pallas import tpu as pltpu
from jax.sharding import PartitionSpec as P

MESH = pl.DeviceIdType.MESH
HD = 128
CAP = 8
X, Y, Z, LINE, CORES = 4, 4, 16, 8, 2
PLANE = X * Y * CORES
SUB = 4
CHUNKS = 4
BATCH = 2 * CAP
STEPS = 2 * CHUNKS
EPSILON = 1e-06
NEG = -1e30
ANY = pl.BlockSpec(memory_space=pl.ANY)
VMEM = pl.BlockSpec(memory_space=pltpu.VMEM)


def place():
    s = lax.axis_index("seq")
    e = lax.axis_index("exp")
    c = e % 2
    y = (e // 2) % Y
    zh = (e // (2 * Y)) % 2
    x = e // (4 * Y)
    return x, y, zh * LINE + s, c


def device(x, y, z, c):
    x, y, z = x % X, y % Y, z % Z
    return {"seq": z % LINE, "exp": ((x * 2 + z // LINE) * Y + y) * 2 + c}


def rows(start, count):
    return pl.ds(pl.multiple_of(start, 16), count)


def layer_kernel(
    q_hbm, k_hbm, v_hbm, span_hbm, res_hbm, gain_hbm, logits_hbm, ids_hbm, keep_hbm, wout_ref, wg_ref, wu_ref, wd_ref,
    hidden_ref, out_ref,
    q_ref, kv, span_ref, res_ref, gain_ref, logits_ref, ids_ref, keep_ref, meta, metas,
    wbuf, att, total, wv, pick, comb, tok, sent, got, accum, act, made, back, own, far, home,
    send, recv, local,
    z_send, z_recv, h_send, h_recv, p_send, p_recv, r_send, r_recv, f_send, f_recv, o_send, o_recv,
):
    x, y, z, c = place()
    s = z % LINE
    zh = z // LINE
    p = z % SUB
    me = (x * Y + y) * CORES + c
    width = tok.shape[2]

    def at(dx=0, dy=0, dz=0):
        return device(x + dx + X, y + dy + Y, z + dz + Z, c)

    def partner(o):
        dx = o % X
        px = (x + dx) % X
        py = (y + o // (X * CORES) + dx) % Y
        pc = (c + o // X) % CORES
        return (px * Y + py) * CORES + pc, device(px, py, z, pc)

    sibling = device(x, y, z, 1 - c)
    counter = [0]

    def remote(src, dst, peer):
        i = counter[0]
        counter[0] += 1
        return copy_to(src, dst, send.at[i], recv.at[i], peer)

    def copy_to(src, dst, ss, rs, peer):
        return pltpu.make_async_remote_copy(
            src_ref=src, dst_ref=dst, send_sem=ss, recv_sem=rs, device_id=peer, device_id_type=MESH
        )

    def block(m, owner):
        return wv.at[m, rows(96 * ((owner + SUB) % SUB), 96)]

    ja = (y * 2 + c) * X + x
    jb = (x * 2 + c) * Y + y

    def slice_piece(d):
        t = (s - d + LINE) % LINE
        return wbuf.at[t, rows(jnp.where(t < 4, ja, jb) * 16, 16)]

    mine = jnp.where(s < 4, ja, jb) * 16
    piece = slice_piece(0)
    moves = [
        (k_hbm, kv.at[4, 0]), (v_hbm, kv.at[4, 1]), (wout_ref.at[rows(mine, 16)], piece),
        (ids_hbm, ids_ref), (keep_hbm, keep_ref), (logits_hbm, logits_ref), (span_hbm, span_ref),
        (wg_ref, wv.at[0, rows(96 * p, 96)]), (wu_ref, wv.at[1, rows(96 * p, 96)]),
        (wd_ref, wv.at[2, rows(96 * p, 96)]),
        (q_hbm, q_ref), (res_hbm, res_ref), (gain_hbm, gain_ref),
    ]
    loads = [pltpu.make_async_copy(src, dst, local.at[i]) for i, (src, dst) in enumerate(moves)]
    for load in loads:
        load.start()

    barrier = pltpu.get_barrier_semaphore()
    for d in (1, -1, 2, -2, 3, -3, 4, -4, 8):
        pl.semaphore_signal(barrier, inc=1, device_id=at(dz=d), device_id_type=MESH)

    def greet(o, _):
        pl.semaphore_signal(barrier, inc=1, device_id=partner(o)[1], device_id_type=MESH)
        return 0

    lax.fori_loop(1, PLANE, greet, 0)
    pl.semaphore_wait(barrier, 9 + PLANE - 1)

    kv_steps = [remote(kv.at[4 - d], kv.at[3 - d], at(dz=1)) for d in range(4)]
    z_up = [remote(slice_piece(d), slice_piece(d), at(dz=1)) for d in range(4)]
    z_down = [remote(slice_piece(-d), slice_piece(-d), at(dz=-1)) for d in range(3)]
    z_copies = z_up + z_down
    for load in loads[:3]:
        load.wait()
    z_up[0].start()
    z_down[0].start()
    kv_steps[0].start()

    for load in loads[3:7]:
        load.wait()
    z_up[0].wait_recv()
    z_up[1].start()
    z_down[0].wait_recv()
    z_down[1].start()
    experts = logits_ref.shape[1]
    expert = lax.broadcasted_iota(jnp.int32, (experts, 64), 0)
    named = expert == ids_ref[0:1, :]
    kept = named & (keep_ref[0:1, :] == 1)
    for k in range(1, ids_ref.shape[0]):
        hit = expert == ids_ref[k:k + 1, :]
        named = named | hit
        kept = kept | (hit & (keep_ref[k:k + 1, :] == 1))
    earlier = lax.broadcasted_iota(jnp.int32, (64, 64), 0) < lax.broadcasted_iota(jnp.int32, (64, 64), 1)
    before = jnp.dot(
        jnp.where(kept, 1.0, 0.0).astype(jnp.bfloat16),
        jnp.where(earlier, 1.0, 0.0).astype(jnp.bfloat16),
        preferred_element_type=jnp.float32,
    )
    slot = jnp.where(kept, before, -1.0)
    same = lax.broadcasted_iota(jnp.int32, (64, 64), 0) == lax.broadcasted_iota(jnp.int32, (64, 64), 1)
    identity = jnp.where(same, 1.0, 0.0).astype(jnp.bfloat16)
    rest = logits_ref[...]
    logits = jnp.zeros((experts, 64), jnp.float32)
    for _ in range(3):
        high = rest.astype(jnp.bfloat16)
        rest = rest - high.astype(jnp.float32)
        logits = logits + lax.dot_general(
            high, identity, (((0,), (0,)), ((), ())), preferred_element_type=jnp.float32
        )
    chosen = jnp.where(named, logits, -jnp.inf)
    terms = jnp.exp(chosen - jnp.max(chosen, axis=0, keepdims=True))
    weight = jnp.where(kept, terms / jnp.sum(terms, axis=0, keepdims=True), 0.0)
    z_up[1].wait_recv()
    z_up[2].start()
    z_down[1].wait_recv()
    z_down[2].start()
    slot = jnp.concatenate([slot, slot], axis=1)
    weight = jnp.concatenate([weight, weight], axis=1)
    group = Y * CORES
    for half in range(2):
        for i in range(X):
            chunk = slice(group * (2 * i + half), group * (2 * i + half + 1))
            meta[half, group * i:group * (i + 1)] = slot[chunk]
            meta[half, PLANE + group * i:PLANE + group * (i + 1)] = weight[chunk]
    metas[0] = meta[zh]
    meta_copies = [
        remote(meta.at[1 - zh], metas.at[1], at(dz=8)),
        remote(meta.at[((z + 4) % Z) // LINE], metas.at[2], at(dz=4)),
        remote(meta.at[((z + 12) % Z) // LINE], metas.at[3], at(dz=-4)),
    ]
    for copy in meta_copies:
        copy.start()

    z_up[2].wait_recv()
    z_up[3].start()
    z_down[2].wait_recv()
    kv_steps[0].wait_recv()
    kv_steps[1].start()
    z_up[3].wait_recv()

    up1 = [remote(block(m, p), block(m, p), at(dz=1)) for m in range(3)]
    down1 = [remote(block(m, p), block(m, p), at(dz=-1)) for m in range(3)]
    up2 = [remote(block(m, p - 1), block(m, p - 1), at(dz=1)) for m in range(3)]
    down2 = [remote(block(m, p + 1), block(m, p + 1), at(dz=-1)) for m in range(3)]
    up3 = [remote(block(m, 0), block(m, 0), at(dz=1)) for m in range(3)]
    down3 = [remote(block(m, 3), block(m, 3), at(dz=-1)) for m in range(3)]

    def pass_on(m):
        pl.when(p > 0)(up1[m].wait_recv)
        pl.when(p < 3)(down1[m].wait_recv)
        pl.when((p > 0) & (p < 3))(up2[m].start)
        pl.when((p > 0) & (p < 3))(down2[m].start)

    def pass_last(m):
        pl.when(p > 1)(up2[m].wait_recv)
        pl.when(p < 2)(down2[m].wait_recv)
        pl.when(p == 2)(up3[m].start)
        pl.when(p == 1)(down3[m].start)

    def piece_a(dx, dy, lo, n):
        return wbuf.at[pl.ds(lo, n), rows(16 * ((((y + dy + Y) % Y) * 2 + c) * X + (x + dx + X) % X), 16)]

    def piece_b(dx, dy, lo, n):
        return wbuf.at[pl.ds(4 + lo, n), rows(16 * ((((x + dx + X) % X) * 2 + c) * Y + (y + dy + Y) % Y), 16)]

    def lap(region, step):
        first = [remote(region(0, 0, 4), region(0, 0, 4), step(d)) for d in (1, -1)]
        second = [
            remote(region(-1, 0, 2), region(-1, 0, 2), step(1)),
            remote(region(1, 2, 2), region(1, 2, 2), step(-1)),
        ]
        return first, second

    step_x = lambda d: at(dx=d)
    step_y = lambda d: at(dy=d)
    a1, a2 = lap(lambda d, lo, n: piece_a(d, 0, lo, n), step_x)
    b1, b2 = lap(lambda d, lo, n: piece_b(0, d, lo, n), step_y)
    second_a = {o: lap(lambda d, lo, n, o=o: piece_a(o, d, lo, n), step_y) for o in (0, 1, -1, 2)}
    second_b = {o: lap(lambda d, lo, n, o=o: piece_b(d, o, lo, n), step_x) for o in (0, 1, -1, 2)}
    c1 = {o: second_a[o][0] + second_b[o][0] for o in second_a}
    c2 = {o: second_a[o][1] + second_b[o][1] for o in second_a}

    def lane_a(d):
        return wbuf.at[pl.ds(0, 4), rows(64 * (((y + d + Y) % Y) * 2 + c), 64)]

    def lane_b(d):
        return wbuf.at[pl.ds(4, 4), rows(64 * (((x + d + X) % X) * 2 + c), 64)]

    twins = {d: [remote(lane_a(d), lane_a(d), sibling), remote(lane_b(d), lane_b(d), sibling)] for d in (0, 1, -1, 2)}
    for copy in a1 + b1 + c1[0]:
        copy.start()
    for load in loads[7:10]:
        load.wait()
    for m in range(3):
        pl.when(p < 3)(up1[m].start)
        pl.when(p > 0)(down1[m].start)
    for copy in a1 + b1:
        copy.wait_recv()
    for copy in a2 + b2 + c1[1] + c1[-1]:
        copy.start()
    kv_steps[1].wait_recv()
    kv_steps[2].start()
    for copy in c1[0]:
        copy.wait_recv()
    for copy in c2[0]:
        copy.start()
    for copy in a2 + b2:
        copy.wait_recv()
    for copy in c1[2] + twins[0]:
        copy.start()
    kv_steps[2].wait_recv()
    kv_steps[3].start()

    for copy in meta_copies:
        copy.wait_recv()
    for a in range(2):
        lane = lax.broadcasted_iota(jnp.int32, (PLANE, 128), 1)
        slots = jnp.where(lane < 64, metas[2 * a, 0:PLANE], metas[2 * a + 1, 0:PLANE])
        weights = jnp.where(lane < 64, metas[2 * a, PLANE:], metas[2 * a + 1, PLANE:])
        row = lax.broadcasted_iota(jnp.int32, (PLANE, BATCH, 128), 1)
        column = lax.broadcasted_iota(jnp.int32, (PLANE, BATCH, 128), 2)
        hit = (row // CAP == column // 64) & (slots[:, None, :] == (row % CAP).astype(jnp.float32))
        pick[a] = jnp.where(hit, 1.0, 0.0).reshape(PLANE * BATCH, 128).astype(jnp.bfloat16)
        comb[a] = jnp.where(hit, weights[:, None, :], 0.0).reshape(PLANE * BATCH, 128).astype(jnp.bfloat16)

    docs = lax.broadcasted_iota(jnp.int32, (8, 320), 0)
    key_doc = jnp.where(docs == span_ref[...], 1.0, 0.0).astype(jnp.bfloat16)
    same_doc = lax.dot_general(
        key_doc[:, 256:320], key_doc, (((0,), (0,)), ((), ())), preferred_element_type=jnp.float32
    )
    key_at = lax.broadcasted_iota(jnp.int32, (64, 320), 1)
    query_at = lax.broadcasted_iota(jnp.int32, (64, 320), 0)
    bias = jnp.where((key_at <= query_at + 256) & (same_doc > 0.5), 0.0, NEG)
    loads[10].wait()

    def attend(g):
        head = lambda h: (g * 8 + h) * HD
        queries = jnp.concatenate([q_ref[:, head(h):head(h) + HD] for h in range(8)], axis=0)
        keys = kv[:, 0, :, g * HD:(g + 1) * HD].reshape(5 * 64, HD)
        values = kv[:, 1, :, g * HD:(g + 1) * HD].reshape(5 * 64, HD)
        scores = lax.dot_general(
            queries, keys, (((1,), (1,)), ((), ())), preferred_element_type=jnp.float32
        ) * (1.0 / HD**0.5)
        scores = (scores.reshape(8, 64, 320) + bias[None]).reshape(512, 320)
        terms = jnp.exp(scores - jnp.max(scores, axis=-1, keepdims=True))
        probs = (terms / jnp.sum(terms, axis=-1, keepdims=True)).astype(jnp.bfloat16)
        out = jnp.dot(probs, values, preferred_element_type=jnp.float32).astype(jnp.bfloat16)
        for h in range(8):
            att[:, head(h):head(h) + HD] = out[64 * h:64 * (h + 1)]

    for copy in c1[1] + c1[-1]:
        copy.wait_recv()
    for copy in c2[1] + c2[-1]:
        copy.start()
    pass_on(0)
    for copy in c1[2]:
        copy.wait_recv()
    for copy in c2[2] + twins[1] + twins[-1]:
        copy.start()
    pass_on(1)
    kv_steps[3].wait_recv()
    for g in range(4):
        attend(g)
    for o in c2:
        for copy in c2[o]:
            copy.wait_recv()
    for copy in twins[2]:
        copy.start()
    pass_on(2)
    for d in (0, 1, -1, 2):
        for copy in twins[d]:
            copy.wait_recv()

    for load in loads[11:]:
        load.wait()
    for n in range(4):
        cols = slice(512 * n, 512 * (n + 1))
        acc = res_ref[:, cols].astype(jnp.float32)
        for t in range(8):
            acc = acc + jnp.dot(
                att[:, 512 * t:512 * (t + 1)], wbuf[t, :, cols], preferred_element_type=jnp.float32
            )
        total[:, cols] = acc
    hidden = total[...]
    square = jnp.mean(hidden * hidden, axis=-1, keepdims=True)
    normed = (hidden * lax.rsqrt(square + EPSILON) * gain_ref[...]).astype(jnp.bfloat16)
    for q in range(CHUNKS):
        tok[q, 0:64] = normed[:, width * q:width * (q + 1)]

    near = [
        (
            copy_to(tok.at[q, pl.ds(0, 64)], tok.at[q, pl.ds(128, 64)], z_send.at[q, 0], z_recv.at[q, 0], at(dz=4)),
            copy_to(tok.at[q, pl.ds(0, 64)], tok.at[q, pl.ds(192, 64)], z_send.at[q, 1], z_recv.at[q, 1], at(dz=-4)),
        )
        for q in range(CHUNKS)
    ]
    across = [
        (
            copy_to(tok.at[q, pl.ds(128, 32)], tok.at[q, pl.ds(64, 32)], h_send.at[q, 0], h_recv.at[q, 0], at(dz=4)),
            copy_to(tok.at[q, pl.ds(224, 32)], tok.at[q, pl.ds(96, 32)], h_send.at[q, 1], h_recv.at[q, 1], at(dz=-4)),
        )
        for q in range(CHUNKS)
    ]
    for copy in near[0]:
        copy.start()
    hidden_ref[...] = hidden.astype(jnp.bfloat16)

    def spread(src, dst, i, ss, rs):
        def go(o, _):
            peer, where = partner(o)
            copy_to(
                src.at[i, rows(BATCH * peer, BATCH)], dst.at[i, rows(BATCH * me, BATCH)], ss.at[i], rs.at[i], where
            ).start()
            return 0

        lax.fori_loop(1, PLANE, go, 0)
        dst[i, rows(BATCH * me, BATCH)] = src[i, rows(BATCH * me, BATCH)]

    def whole(src, dst, i, ss, rs):
        every = pl.ds(0, BATCH * (PLANE - 1))
        return copy_to(src.at[i, every], dst.at[i, every], ss.at[i], rs.at[i], at(dz=1))

    def tile_rows(i):
        return pl.ds(pl.multiple_of(i * 256, 256), 256)

    def dispatch(b, q):
        def tile(i, _):
            sent[b * CHUNKS + q, tile_rows(i)] = jnp.dot(
                pick[b, tile_rows(i)], tok[q, 128 * b:128 * (b + 1)], preferred_element_type=jnp.float32
            ).astype(jnp.bfloat16)
            return 0

        lax.fori_loop(0, 2, tile, 0)
        spread(sent, got, b * CHUNKS + q, p_send, p_recv)

    for q in range(CHUNKS):
        if q < CHUNKS - 1:
            for copy in near[q]:
                copy.wait_send()
            for copy in near[q + 1]:
                copy.start()
        for copy in near[q]:
            copy.wait_recv()
        for copy in across[q]:
            copy.start()
        dispatch(1, q)
        if q >= 1:
            for copy in across[q - 1]:
                copy.wait_recv()
            dispatch(0, q - 1)
    for copy in across[CHUNKS - 1]:
        copy.wait_recv()
    dispatch(0, CHUNKS - 1)
    for m in range(3):
        pass_last(m)

    def last_here(m):
        pl.when(p == 3)(up3[m].wait_recv)
        pl.when(p == 0)(down3[m].wait_recv)

    last_here(0)
    last_here(1)
    transposed = (((1,), (1,)), ((), ()))

    def gate_up(b, q):
        step = b * CHUNKS + q
        whole(sent, got, step, p_send, p_recv).wait_recv()
        cols = slice(width * q, width * (q + 1))

        def tile(i, _):
            for m in range(2):
                value = lax.dot_general(
                    got[step, tile_rows(i)], wv[m, :, cols], transposed, preferred_element_type=jnp.float32
                )
                if q == 0:
                    accum[b, m, tile_rows(i)] = value
                else:
                    accum[b, m, tile_rows(i)] += value
            return 0

        lax.fori_loop(0, 2, tile, 0)

    def activate(b):
        def tile(i, _):
            gate = accum[b, 0, tile_rows(i)]
            act[b, tile_rows(i)] = (gate / (1.0 + jnp.exp(-gate)) * accum[b, 1, tile_rows(i)]).astype(jnp.bfloat16)
            return 0

        lax.fori_loop(0, 2, tile, 0)

    def down(b, q):
        cols = slice(width * q, width * (q + 1))

        def tile(i, _):
            made[b * CHUNKS + q, tile_rows(i)] = jnp.dot(
                act[b, tile_rows(i)], wv[2, :, cols], preferred_element_type=jnp.float32
            ).astype(jnp.bfloat16)
            return 0

        lax.fori_loop(0, 2, tile, 0)

    def give_back(step):
        if step > 0:
            whole(made, back, step - 1, r_send, r_recv).wait_send()
        spread(made, back, step, r_send, r_recv)

    def half_copies(q):
        return (
            copy_to(far.at[q, 0, pl.ds(0, 32)], home.at[q, 0, pl.ds(0, 32)], f_send.at[q, 0], f_recv.at[q, 0], at(dz=4)),
            copy_to(far.at[q, 0, pl.ds(32, 32)], home.at[q, 0, pl.ds(32, 32)], f_send.at[q, 1], f_recv.at[q, 1], at(dz=-4)),
        )

    def home_copies(q):
        return (
            copy_to(far.at[q, 1], home.at[q, 1], o_send.at[q, 0], o_recv.at[q, 0], at(dz=-4)),
            copy_to(far.at[q, 2], home.at[q, 2], o_send.at[q, 1], o_recv.at[q, 1], at(dz=4)),
        )

    def combine(b, q):
        step = b * CHUNKS + q
        whole(made, back, step, r_send, r_recv).wait_recv()
        part = lax.dot_general(
            comb[b], back[step], (((0,), (0,)), ((), ())), preferred_element_type=jnp.float32
        )
        if b == 0:
            own[q] = part[0:64]
            far[q, 0] = part[64:128].astype(jnp.bfloat16)
            for copy in half_copies(q):
                copy.start()
        else:
            for copy in half_copies(q):
                copy.wait_recv()
            far[q, 1, 0:32] = part[0:32].astype(jnp.bfloat16)
            far[q, 1, 32:64] = (part[32:64] + home[q, 0, 32:64].astype(jnp.float32)).astype(jnp.bfloat16)
            far[q, 2, 0:32] = (part[64:96] + home[q, 0, 0:32].astype(jnp.float32)).astype(jnp.bfloat16)
            far[q, 2, 32:64] = part[96:128].astype(jnp.bfloat16)
            for copy in home_copies(q):
                copy.start()

    def finish(q):
        for copy in home_copies(q):
            copy.wait_recv()
        total = own[q] + home[q, 1].astype(jnp.float32) + home[q, 2].astype(jnp.float32)
        out_ref[:, width * q:width * (q + 1)] = total.astype(jnp.bfloat16)

    for q in range(CHUNKS):
        gate_up(1, q)
        gate_up(0, q)
    activate(0)
    last_here(2)
    down(0, 0)
    give_back(0)
    for q in range(1, CHUNKS):
        down(0, q)
    give_back(1)
    activate(1)
    give_back(2)
    combine(0, 0)
    down(1, 0)
    down(1, 1)
    give_back(3)
    combine(0, 1)
    down(1, 2)
    down(1, 3)
    give_back(4)
    combine(0, 2)
    give_back(5)
    combine(0, 3)
    give_back(6)
    combine(1, 0)
    give_back(7)
    combine(1, 1)
    finish(0)
    combine(1, 2)
    finish(1)
    combine(1, 3)
    finish(2)
    finish(3)

    for copy in near[CHUNKS - 1]:
        copy.wait_send()
    for q in range(CHUNKS):
        for copy in across[q] + half_copies(q) + home_copies(q):
            copy.wait_send()
    for step in range(STEPS):
        whole(sent, got, step, p_send, p_recv).wait_send()
    whole(made, back, STEPS - 1, r_send, r_recv).wait_send()
    for copy in kv_steps + z_copies + meta_copies + a1 + b1 + a2 + b2:
        copy.wait_send()
    for o in c1:
        for copy in c1[o] + c2[o] + twins[o]:
            copy.wait_send()
    for m in range(3):
        pl.when(p < 3)(up1[m].wait_send)
        pl.when(p > 0)(down1[m].wait_send)
        pl.when((p > 0) & (p < 3))(up2[m].wait_send)
        pl.when((p > 0) & (p < 3))(down2[m].wait_send)
        pl.when(p == 2)(up3[m].wait_send)
        pl.when(p == 1)(down3[m].wait_send)


def layer(*args):
    d = args[4].shape[1]
    width = d // CHUNKS
    slots = PLANE * BATCH
    units = SUB * 96
    dma = lambda *shape: pltpu.SemaphoreType.DMA(shape)
    half = lambda *shape: pltpu.VMEM(shape, jnp.bfloat16)
    full = lambda *shape: pltpu.VMEM(shape, jnp.float32)
    return pl.pallas_call(
        layer_kernel,
        out_shape=(jax.ShapeDtypeStruct((64, d), jnp.bfloat16), jax.ShapeDtypeStruct((64, d), jnp.bfloat16)),
        in_specs=[ANY] * len(args),
        out_specs=(VMEM, VMEM),
        scratch_shapes=[
            half(64, 4096), half(5, 2, 64, 512), pltpu.VMEM((1, 320), jnp.int32), half(64, d), full(1, d),
            full(64, 64), pltpu.VMEM((8, 64), jnp.int32), pltpu.VMEM((8, 64), jnp.int32),
            full(2, 64, 128), full(4, 64, 128),
            half(LINE, 512, d), half(64, 4096), full(64, d), half(3, units, d),
            half(2, slots, 128), half(2, slots, 128), half(CHUNKS, 256, width),
            half(STEPS, slots, width), half(STEPS, slots, width),
            full(2, 2, slots, units), half(2, slots, units),
            half(STEPS, slots, width), half(STEPS, slots, width),
            full(CHUNKS, 64, width), half(CHUNKS, 3, 64, width), half(CHUNKS, 3, 64, width),
            dma(96), dma(96), dma(13),
            dma(CHUNKS, 2), dma(CHUNKS, 2), dma(CHUNKS, 2), dma(CHUNKS, 2),
            dma(STEPS), dma(STEPS), dma(STEPS), dma(STEPS),
            dma(CHUNKS, 2), dma(CHUNKS, 2), dma(CHUNKS, 2), dma(CHUNKS, 2),
        ],
        compiler_params=pltpu.CompilerParams(
            collective_id=0, has_side_effects=True, vmem_limit_bytes=60 * 2**20
        ),
        cost_estimate=pl.CostEstimate(flops=7 * 10**9, bytes_accessed=3 * 10**7, transcendentals=10**6),
    )(*args)


def shards(
    queries, key_heads, value_heads, doc_ids, residual, w_out, norm_gain, router_logits, expert_ids, keep_mask,
    w_gate, w_up, w_down,
):
    s = lax.axis_index("seq")
    doc = jnp.pad(doc_ids[0], (256, 0), constant_values=-1)
    span = lax.dynamic_slice(doc, (64 * s,), (320,))[None]
    hidden, out = layer(
        queries[0], key_heads[0], value_heads[0], span, residual[0], norm_gain[None], router_logits[0],
        expert_ids[0].T, keep_mask[0].T, w_out, w_gate[0], w_up[0], w_down[0],
    )
    return hidden[None], out[None]


def solution(mesh):
    split = P("exp", "seq", None)
    return jax.shard_map(
        shards,
        mesh=mesh,
        in_specs=(split, split, split, P("exp", None), split, P("seq", None), P()) + (split,) * 6,
        out_specs=(split, split),
        check_vma=False,
    )
```
